256 devices in a mesh: rep: 16 (over x, y), fsdp: 16 (over z, core).
Axes of the slice: x: 4, y: 4, z: 8, core: 2. Of those that a mesh axis runs over, the one named last changes fastest.
Arguments:
- grads: bfloat16 [256, 704, 1024], P(None, 'fsdp', 'rep')
- momentum: bfloat16 [256, 2, 704, 1024], P(('rep', 'fsdp')), may hold values from -6 to 6
- owner: int32 [256], replicated, may hold values from 0 to 255, as said below
Outputs:
- update: bfloat16 [256, 704, 1024], P(None, 'fsdp', 'rep')
- new_momentum: bfloat16 [256, 2, 704, 1024], P(('rep', 'fsdp'))
The draws below stay inside these ranges and needn't reach their ends.
Inputs may be any that keep to these rules, and one draw needn't show every extreme that they name: `owner`: every device owns at most 2 matrices, and some device owns exactly 2.
All inputs are finite; a program needn't handle non-finite values.
Results may differ from the reference program's by a relative error of at most 0.0066.
Values may be sent and summed in bfloat16 or wider, within the bound.
A program may use at most 128 MiB of HBM per device.

```python
import jax
import jax.numpy as jnp
from jax import lax

HID = 704
D = 1024
ITERS = 2
SLOTS = 2
MATS = 256
DEVICES = 256


def draw_grads(key, part):
    key = jax.random.fold_in(key, 11)
    base_key, row_key, col_key = jax.random.split(key, 3)
    row_scale = jnp.exp(jax.random.uniform(row_key, (MATS, HID, 1), jnp.float32) * jnp.log(10.0))
    col_scale = jnp.exp(jax.random.uniform(col_key, (MATS, 1, D), jnp.float32) * jnp.log(10.0))
    noise = jax.random.normal(base_key, (MATS, HID, D), jnp.float32)
    return (noise * row_scale * col_scale / 16.0).astype(jnp.bfloat16)


def draw_owner(key, part):
    key = jax.random.fold_in(key, 23)
    perm_key, order_key = jax.random.split(key)
    devices_perm = jax.random.permutation(perm_key, DEVICES).astype(jnp.int32)
    doubled = DEVICES // 4
    listing = jnp.concatenate([devices_perm[:doubled], devices_perm[:DEVICES - doubled]])
    order = jax.random.permutation(order_key, DEVICES)
    return listing[order].astype(jnp.int32)


def block_levels(own_key, extent, pieces, smallest, top_value):
    def one(position, shards_of):
        steps = jax.random.uniform(jax.random.fold_in(jax.random.fold_in(own_key, 6), position), (shards_of,), jnp.float32, smallest / len(pieces), top_value / len(pieces))
        return jnp.repeat(jnp.exp(steps), extent[position] // shards_of).reshape((-1,) + (1,) * (len(extent) - position - 1))

    loudness = one(*pieces[0])
    for cut in pieces[1:]:
        loudness = loudness * one(*cut)
    return loudness


def gaussian(own_key, extent, deviation, limit, cuts=(), held_as=jnp.bfloat16):
    loudness = block_levels(own_key, extent, cuts, -0.22, 0.18) if cuts else 1.0
    entries = jax.random.normal(own_key, extent, jnp.float32) * deviation * loudness
    return jnp.minimum(jnp.maximum(entries, -limit), limit).astype(held_as)


def setup_inputs(seed: int = 0) -> dict:
    keys = jax.random.split(jax.random.key(seed), 4)
    grads = draw_grads(jax.random.fold_in(keys[3], 71), 0)
    momentum = gaussian(keys[1], (DEVICES, SLOTS, HID, D), 1.0, 6.0, ((0, 256),))
    owner = draw_owner(jax.random.fold_in(keys[3], 71), 0)
    return dict(grads=grads, momentum=momentum, owner=owner)


def slots_of(owner):
    order = jnp.arange(owner.shape[0], dtype=jnp.int32)
    earlier = (owner[:, None] == owner[None, :]) & (order[None, :] < order[:, None])
    return lax.optimization_barrier(jnp.sum(earlier.astype(jnp.int32), axis=1)).astype(jnp.int32)

def orthogonalize(pair):
    grad, previous = pair
    moment = (0.95 * previous.astype(jnp.float32) + grad.astype(jnp.float32)).astype(jnp.bfloat16)
    nesterov = grad.astype(jnp.float32) + 0.95 * lax.optimization_barrier(moment).astype(jnp.float32)
    total = jnp.sum(nesterov * nesterov)
    current = (nesterov / (jnp.sqrt(total) + 1e-07)).astype(jnp.bfloat16)
    for turn in range(ITERS):
        gram = jnp.dot(current, current.T, preferred_element_type=jnp.float32).astype(jnp.bfloat16)
        square = jnp.dot(gram, gram, preferred_element_type=jnp.float32)
        mixed = (-4.775 * lax.optimization_barrier(gram).astype(jnp.float32) + 2.0315 * square).astype(jnp.bfloat16)
        product = jnp.dot(mixed, current, preferred_element_type=jnp.float32)
        current = (3.4445 * lax.optimization_barrier(current).astype(jnp.float32) + product).astype(jnp.bfloat16)
    factor = 0.2 * max(HID, D) ** 0.5
    result = (factor * lax.optimization_barrier(current).astype(jnp.float32)).astype(jnp.bfloat16)
    return (result, moment)

def reference(grads, momentum, owner):
    slot = slots_of(owner)
    previous = momentum[owner, slot]
    update, moment = lax.map(orthogonalize, (grads, previous))
    new_momentum = momentum.at[owner, slot].set(moment)
    return (update, new_momentum)
```

```python
import functools

import jax
import jax.numpy as jnp
import numpy as np
from jax import lax
from jax.experimental import pallas as pl
from jax.experimental.pallas import tpu as pltpu
from jax.sharding import PartitionSpec as P

ITERS = 2
MESH = pl.DeviceIdType.MESH
BF = jnp.bfloat16
F32 = jnp.float32


def mm(a, b, dims=((1,), (0,))):
    return lax.dot_general(a, b, (dims, ((), ())), preferred_element_type=F32)


def wait_bytes(ref, sem):
    pltpu.make_async_copy(ref, ref, sem).wait()


def tile_cols(n, size):
    return pl.ds(pl.multiple_of(n * size, size), size)


def kernel(
    cfg,
    owner_ref, g_hbm, mom_hbm, regroup_hbm, regroup_t_hbm, rows_hbm, rows_t_hbm, swap_hbm,
    upd_ref, new_hbm,
    g, regroup, regroup_t, rows, rows_t, swap, keys,
    s_buf, t_buf, v_buf, w_buf, u_buf, mom, new, zp, nest, x, gram, mixed,
    load_sem, mom_sem, new_sem, in_send, in_recv, out_send, out_recv,
):
    nr, nf, half, hid, width, pad = cfg
    rep, fs = lax.axis_index("rep"), lax.axis_index("fsdp")
    mats = nr * nf
    blk = half + 2
    upper = nf * blk

    loads = [(g_hbm, g), (regroup_hbm, regroup), (swap_hbm, swap), (rows_hbm, rows),
             (rows_t_hbm, rows_t), (regroup_t_hbm, regroup_t)]
    loads = [pltpu.make_async_copy(a, b, load_sem.at[i]) for i, (a, b) in enumerate(loads)]
    for load in loads:
        load.start()
    for s in range(2):
        pltpu.make_async_copy(mom_hbm.at[s], mom.at[s], mom_sem.at[s]).start()

    def others(first, last, visit):
        @pl.loop(first, last)
        def _(k):
            to_f = lax.rem(fs + k, nf)

            @pl.loop(0, nr)
            def _(j):
                visit(lax.rem(rep + j, nr), to_f)

    def own_row(visit):
        @pl.loop(1, nr)
        def _(j):
            visit(lax.rem(rep + j, nr), fs)

    barrier = pltpu.get_barrier_semaphore()

    def greet(to_r, to_f):
        pl.semaphore_signal(barrier, inc=1, device_id=(to_r, to_f), device_id_type=MESH)

    own_row(greet)
    others(1, nf, greet)

    owner = owner_ref[...]
    down = jnp.transpose(jnp.broadcast_to(owner, (mats, mats)))
    index = lax.broadcasted_iota(jnp.int32, (mats, mats), 0)
    order = lax.broadcasted_iota(jnp.int32, (mats, mats), 1)
    earlier = jnp.where((down == owner) & (index < order), 1, 0)
    slot = jnp.sum(earlier, axis=0, keepdims=True)
    place = (owner % nf) * nr + owner // nf
    keys[0:1, :] = jnp.where(slot == 0, place, -1)
    keys[1:2, :] = jnp.where(slot == 1, place, -1)

    def select(s):
        slot_id = lax.broadcasted_iota(jnp.int32, (mats, mats), 0)
        return jnp.where(slot_id == keys[s : s + 1, :], 1.0, 0.0).astype(BF)

    def gather(s):
        chosen = select(s)

        @pl.loop(0, half)
        def _(a):
            both = jnp.concatenate([g[a], g[a + half]], axis=0)
            out = mm(chosen, both, ((1,), (1,))).astype(BF)
            s_buf[s, :, a] = out.reshape(nf, nr, 128)

    def send_in(s):
        def regroup_two(k):
            first, second = lax.rem(fs + k, nf), lax.rem(fs + k + 1, nf)
            pair = jnp.concatenate(
                [s_buf[s, first].reshape(half * nr, 128), s_buf[s, second].reshape(half * nr, 128)], axis=1
            )
            out = mm(regroup[...], pair)
            t_buf[s, pl.ds(first * nr, nr)] = out[:, :128].reshape(nr, blk, 128).astype(BF)
            t_buf[s, pl.ds(second * nr, nr)] = out[:, 128:].reshape(nr, blk, 128).astype(BF)

        def send(to_r, to_f):
            pltpu.make_async_remote_copy(
                t_buf.at[s, to_f * nr + to_r], v_buf.at[s, rep * nf + fs], in_send.at[s], in_recv.at[s],
                device_id=(to_r, to_f), device_id_type=MESH,
            ).start()

        regroup_two(0)
        pltpu.make_async_copy(t_buf.at[s, fs * nr + rep], v_buf.at[s, rep * nf + fs], in_recv.at[s]).start()
        own_row(send)
        others(1, 2, send)

        @pl.loop(1, nf // 2)
        def _(k):
            regroup_two(2 * k)
            others(2 * k, 2 * k + 2, send)

    def send_out(s):
        def send(to_r, to_f):
            pltpu.make_async_remote_copy(
                w_buf.at[s, to_r * nf + to_f], u_buf.at[s, fs * nr + rep], out_send.at[s], out_recv.at[s],
                device_id=(to_r, to_f), device_id_type=MESH,
            ).start()

        pltpu.make_async_copy(w_buf.at[s, rep * nf + fs], u_buf.at[s, fs * nr + rep], out_recv.at[s]).start()
        own_row(send)
        others(1, nf, send)

    def assemble(s):
        @pl.loop(0, nr // 2)
        def _(q):
            pair = jnp.concatenate(
                [v_buf[s, pl.ds((2 * q + i) * nf, nf)].reshape(upper, 128) for i in range(2)], axis=1
            )
            out = mm(pair, swap[...]).astype(BF)
            cols = tile_cols(q, 128)
            zp[0:upper, cols] = out[:, :128]
            zp[upper : 2 * upper, cols] = out[:, 128:]

    def orthogonalize(s):
        wait_bytes(mom.at[s], mom_sem.at[s])
        own = rep * nf + fs
        mine = jnp.sum(jnp.where(owner_ref[...] == own, 1, 0), axis=1, keepdims=True)
        owned = mine > s

        def start(n, total):
            cols = tile_cols(n, 256)
            grad = mm(rows[0:hid, :], zp[:, cols])
            before = mom[s, :, cols]
            moment = (0.95 * before.astype(F32) + grad).astype(BF)
            new[s, :, cols] = jnp.where(owned, moment.astype(F32), before.astype(F32)).astype(BF)
            value = grad + 0.95 * moment.astype(F32)
            nest[:, cols] = value
            return total + jnp.sum(value * value, axis=0, keepdims=True)

        total = lax.fori_loop(0, width // 256, start, jnp.zeros((1, 256), F32))
        pltpu.make_async_copy(new.at[s], new_hbm.at[s], new_sem.at[s]).start()
        scale = 1.0 / (jnp.sqrt(jnp.sum(total, axis=1, keepdims=True)) + 1e-07)

        @pl.loop(0, width // 256)
        def _(n):
            cols = tile_cols(n, 256)
            x[0:hid, cols] = (nest[:, cols] * scale).astype(BF)

        if pad > hid:
            x[hid:pad, :] = jnp.zeros((pad - hid, width), BF)

        @pl.loop(0, ITERS)
        def _(turn):
            @pl.loop(0, pad // 256)
            def _(n):
                cols = tile_cols(n, 256)
                gram[:, cols] = mm(x[...], x[cols, :], ((1,), (1,))).astype(BF)

            @pl.loop(0, pad // 256)
            def _(n):
                cols = tile_cols(n, 256)
                part = gram[:, cols]
                square = mm(gram[...], part)
                mixed[:, cols] = (-4.775 * part.astype(F32) + 2.0315 * square).astype(BF)

            @pl.loop(0, width // 256)
            def _(n):
                cols = tile_cols(n, 256)
                part = x[:, cols]
                product = mm(mixed[...], part)
                x[:, cols] = (3.4445 * part.astype(F32) + product).astype(BF)

        factor = 0.2 * max(hid, width) ** 0.5

        @pl.loop(0, width // 256)
        def _(n):
            cols = tile_cols(n, 256)
            result = (factor * x[:, cols].astype(F32)).astype(BF)
            spread = mm(rows_t[...], result).astype(BF)
            for h in range(2):
                q = 2 * n + h
                both = jnp.concatenate(
                    [spread[0:upper, 128 * h : 128 * h + 128], spread[upper : 2 * upper, 128 * h : 128 * h + 128]],
                    axis=1,
                )
                out = mm(both, swap[...])
                w_buf[s, pl.ds(2 * q * nf, nf)] = out[:, :128].reshape(nf, blk, 128).astype(BF)
                w_buf[s, pl.ds((2 * q + 1) * nf, nf)] = out[:, 128:].reshape(nf, blk, 128).astype(BF)

    def ungroup(s):
        @pl.loop(0, nf // 2)
        def _(k):
            pair = jnp.concatenate(
                [u_buf[s, pl.ds((2 * k + i) * nr, nr)].reshape(nr * blk, 128) for i in range(2)], axis=1
            )
            out = mm(regroup_t[...], pair).astype(BF)
            s_buf[s, 2 * k] = out[:, :128].reshape(half, nr, 128)
            s_buf[s, 2 * k + 1] = out[:, 128:].reshape(half, nr, 128)

    loads[0].wait()
    gather(0)
    for load in loads[1:]:
        load.wait()
    pl.semaphore_wait(barrier, mats - 1)
    send_in(0)
    gather(1)
    send_in(1)

    for s in range(2):
        wait_bytes(v_buf.at[s], in_recv.at[s])
        assemble(s)
        orthogonalize(s)
        send_out(s)

    for s in range(2):
        wait_bytes(u_buf.at[s], out_recv.at[s])
        ungroup(s)
    chosen = [select(0), select(1)]

    @pl.loop(0, half)
    def _(a):
        out = sum(mm(s_buf[s, :, a].reshape(mats, 128), chosen[s], ((0,), (0,))) for s in range(2)).astype(BF)
        upd_ref[a] = out[0:64]
        upd_ref[a + half] = out[64:128]

    for s in range(2):
        wait_bytes(t_buf.at[s, pl.ds(0, mats - 1)], in_send.at[s])
        wait_bytes(w_buf.at[s, pl.ds(0, mats - 1)], out_send.at[s])
        wait_bytes(new.at[s], new_sem.at[s])


def one_hot(rows, cols, pairs):
    out = np.zeros((rows, cols), np.float32)
    for i, j in pairs:
        out[i, j] = 1.0
    return jnp.asarray(out, BF)


def on_device(grads, momentum, owner):
    nf, nr = lax.axis_size("fsdp"), lax.axis_size("rep")
    mats, tile_rows, tile_cols = grads.shape
    half = tile_rows // 2
    hid, width = nf * tile_rows, nr * tile_cols
    blk = half + 2
    upper = nf * blk
    pad = 2 * upper

    regroup_pairs = [(r * blk + a, a * nr + r) for r in range(nr) for a in range(half)]
    row_pairs = [
        (tile_rows * f + half * h + a, h * upper + f * blk + a)
        for f in range(nf) for h in range(2) for a in range(half)
    ]
    swap_pairs = [(i * 128 + j * 64 + c, j * 128 + i * 64 + c) for i in range(2) for j in range(2) for c in range(64)]
    flip = lambda pairs: [(j, i) for i, j in pairs]
    regroup = one_hot(nr * blk, half * nr, regroup_pairs)
    regroup_t = one_hot(half * nr, nr * blk, flip(regroup_pairs))
    rows = one_hot(pad, pad, row_pairs)
    rows_t = one_hot(pad, pad, flip(row_pairs))
    swap = one_hot(256, 256, swap_pairs)

    vmem = pl.BlockSpec(memory_space=pltpu.VMEM)
    hbm = pl.BlockSpec(memory_space=pl.ANY)
    cfg = (nr, nf, half, hid, width, pad)
    turned = grads.transpose(1, 2, 0)
    tables = [regroup, regroup_t, rows, rows_t, swap]
    by_f = pltpu.VMEM((2, nf, half, nr, 128), BF)
    tiles = pltpu.VMEM((2, mats, blk, 128), BF)
    update, new = pl.pallas_call(
        functools.partial(kernel, cfg),
        out_shape=(
            jax.ShapeDtypeStruct((tile_rows, tile_cols, mats), BF),
            jax.ShapeDtypeStruct(momentum.shape[1:], BF),
        ),
        in_specs=[vmem] + [hbm] * 7,
        out_specs=(vmem, hbm),
        scratch_shapes=[
            pltpu.VMEM(turned.shape, BF),
            *[pltpu.VMEM(table.shape, BF) for table in tables],
            pltpu.VMEM((2, mats), jnp.int32),
            by_f, tiles, tiles, tiles, tiles,
            pltpu.VMEM((2, hid, width), BF),
            pltpu.VMEM((2, hid, width), BF),
            pltpu.VMEM((pad, width), BF),
            pltpu.VMEM((hid, width), F32),
            pltpu.VMEM((pad, width), BF),
            pltpu.VMEM((pad, pad), BF),
            pltpu.VMEM((pad, pad), BF),
            pltpu.SemaphoreType.DMA((6,)),
            *[pltpu.SemaphoreType.DMA((2,)) for _ in range(6)],
        ],
        compiler_params=pltpu.CompilerParams(
            collective_id=0, has_side_effects=True, vmem_limit_bytes=58 * 1024 * 1024
        ),
        name="muon",
    )(owner[None, :], turned, momentum[0], *tables)
    return (update.transpose(2, 0, 1), new[None])


def solution(mesh):
    return jax.shard_map(
        on_device,
        mesh=mesh,
        in_specs=(P(None, "fsdp", "rep"), P(("rep", "fsdp"), None, None, None), P()),
        out_specs=(P(None, "fsdp", "rep"), P(("rep", "fsdp"), None, None, None)),
        check_vma=False,
    )
```

```python
import functools

import jax
import jax.numpy as jnp
import numpy as np
from jax import lax
from jax.experimental import pallas as pl
from jax.experimental.pallas import tpu as pltpu
from jax.sharding import PartitionSpec as P

ITERS = 2
MESH = pl.DeviceIdType.MESH
BF = jnp.bfloat16
F32 = jnp.float32


def mm(a, b, dims=((1,), (0,))):
    return lax.dot_general(a, b, (dims, ((), ())), preferred_element_type=F32)


def wait_bytes(ref, sem):
    pltpu.make_async_copy(ref, ref, sem).wait()


def tile_cols(n, size):
    return pl.ds(pl.multiple_of(n * size, size), size)


def kernel(
    cfg, relayed,
    owner_ref, g_hbm, mom_hbm, regroup_hbm, regroup_t_hbm, rows_hbm, rows_t_hbm, swap_hbm,
    upd_ref, new_hbm,
    g, regroup, regroup_t, rows, rows_t, swap, keys,
    s_buf, t_buf, v_buf, w_buf, u_buf, mom, spun, new, nest, x, gram, mixed,
    load_sem, mom_sem, new_sem, in_send, in_recv, out_send, out_recv,
    *relay_refs,
):
    nr, nf, half, hid, width, pad = cfg
    rep, fs = lax.axis_index("rep"), lax.axis_index("fsdp")
    mats = nr * nf
    blk = half + 2
    upper = nf * blk
    nz = nf // 2
    z, core = fs // 2, lax.rem(fs, 2)
    lane = rep * nf + core * nz + z
    if relayed:
        (zs_buf, zr_buf, zt_buf, zv_buf, zu_buf, spread_in, spread_out,
         z_send, z_recv, p_send, zo_send, zo_recv, po_send, po_recv) = relay_refs

    loads = [(g_hbm, g), (regroup_hbm, regroup), (swap_hbm, swap), (rows_hbm, rows),
             (rows_t_hbm, rows_t), (regroup_t_hbm, regroup_t)]
    loads = [pltpu.make_async_copy(a, b, load_sem.at[i]) for i, (a, b) in enumerate(loads)]
    for load in loads:
        load.start()
    for s in range(2):
        pltpu.make_async_copy(mom_hbm.at[s], mom.at[s, pl.ds(0, hid)], mom_sem.at[s]).start()

    def others(first, last, visit):
        @pl.loop(first, last)
        def _(k):
            to_f = lax.rem(fs + k, nf)

            @pl.loop(0, nr, unroll=4)
            def _(j):
                visit(lax.rem(rep + j, nr), to_f)

    def own_row(visit):
        @pl.loop(1, nr)
        def _(j):
            visit(lax.rem(rep + j, nr), fs)

    barrier = pltpu.get_barrier_semaphore()

    def greet(to_r, to_f):
        pl.semaphore_signal(barrier, inc=1, device_id=(to_r, to_f), device_id_type=MESH)

    own_row(greet)
    others(1, nf, greet)

    owner = owner_ref[...]
    down = jnp.transpose(jnp.broadcast_to(owner, (mats, mats)))
    index = lax.broadcasted_iota(jnp.int32, (mats, mats), 0)
    order = lax.broadcasted_iota(jnp.int32, (mats, mats), 1)
    earlier = (down == owner) & (index < order)
    slot = jnp.sum(jnp.where(earlier, 1, 0), axis=0, keepdims=True)
    place = (owner % nf) * nr + owner // nf
    keys[0:1, :] = jnp.where(slot == 0, place, -1)
    if relayed:
        plane = jnp.where(slot == 1, (owner % nf) // 2, -1)
        plane_down = jnp.transpose(jnp.broadcast_to(plane, (mats, mats)))
        before = (plane_down == plane) & (index < order)
        rank = jnp.sum(jnp.where(before, 1, 0), axis=0, keepdims=True)
        keys[1:2, :] = jnp.where(slot == 1, plane * nr + rank, -1)
        member = (owner // nf) * 2 + owner % 2 + 1
        wide = half * nr
        column = lax.broadcasted_iota(jnp.int32, (wide, mats), 0) % nr
        here = jnp.where(keys[1:2, :] == z * nr + column, 1.0, 0.0).astype(BF)
        members = jnp.broadcast_to(member, (8, mats)).astype(F32).astype(BF)
        owner_of = mm(members, here, ((1,), (1,)))[0:1, :]
        line = lax.broadcasted_iota(jnp.int32, (2 * nr * blk, wide), 0)
        source = lax.broadcasted_iota(jnp.int32, (2 * nr * blk, wide), 1)
        wanted = (owner_of == (line // blk + 1).astype(F32)) & (line % blk == source // nr)
        wanted = jnp.where(wanted, 1.0, 0.0)
        spread_in[...] = wanted.astype(BF)
        spread_out[...] = jnp.transpose(wanted).astype(BF)
    else:
        keys[1:2, :] = jnp.where(slot == 1, place, -1)

    def select(s):
        places = nz * nr if relayed and s == 1 else mats
        slot_id = lax.broadcasted_iota(jnp.int32, (places, mats), 0)
        return jnp.where(slot_id == keys[s : s + 1, :], 1.0, 0.0).astype(BF)

    def gather(s):
        chosen = select(s)

        @pl.loop(0, half)
        def _(a):
            both = jnp.concatenate([g[a], g[a + half]], axis=0)
            out = mm(chosen, both, ((1,), (1,))).astype(BF)
            if relayed and s == 1:
                zs_buf[:, a] = out.reshape(nz, nr, 128)
            else:
                s_buf[s, :, a] = out.reshape(nf, nr, 128)

    def regroup_two(s, k):
        first, second = lax.rem(fs + k, nf), lax.rem(fs + k + 1, nf)
        pair = jnp.concatenate(
            [s_buf[s, first].reshape(half * nr, 128), s_buf[s, second].reshape(half * nr, 128)], axis=1
        )
        out = mm(regroup[...], pair)
        t_buf[s, pl.ds(first * nr, nr)] = out[:, :128].reshape(nr, blk, 128).astype(BF)
        t_buf[s, pl.ds(second * nr, nr)] = out[:, 128:].reshape(nr, blk, 128).astype(BF)

    def send_in(s, regrouped):
        def send(to_r, to_f):
            pltpu.make_async_remote_copy(
                t_buf.at[s, to_f * nr + to_r], v_buf.at[s, lane], in_send.at[s], in_recv.at[s],
                device_id=(to_r, to_f), device_id_type=MESH,
            ).start()

        if not regrouped:
            regroup_two(s, 0)
        pltpu.make_async_copy(t_buf.at[s, fs * nr + rep], v_buf.at[s, lane], in_recv.at[s]).start()
        own_row(send)
        others(1, 2, send)

        @pl.loop(1, nf // 2)
        def _(k):
            if not regrouped:
                regroup_two(s, 2 * k)
            others(2 * k, 2 * k + 2, send)

    def send_out(s):
        def send(to_r, to_f):
            pltpu.make_async_remote_copy(
                w_buf.at[s, to_r * nf + lax.rem(to_f, 2) * nz + to_f // 2], u_buf.at[s, fs * nr + rep], out_send.at[s], out_recv.at[s],
                device_id=(to_r, to_f), device_id_type=MESH,
            ).start()

        pltpu.make_async_copy(w_buf.at[s, lane], u_buf.at[s, fs * nr + rep], out_recv.at[s]).start()
        own_row(send)
        others(1, nf, send)

    def spin_momentum(s):
        wait_bytes(mom.at[s, pl.ds(0, hid)], mom_sem.at[s])
        if pad > hid:
            mom[s, hid:pad, :] = jnp.zeros((pad - hid, width), BF)

        @pl.loop(0, width // 256)
        def _(n):
            cols = tile_cols(n, 256)
            spun[s, :, cols] = mm(rows_t[...], mom[s, :, cols]).astype(BF)

    def store_momentum(s):
        own = rep * nf + fs
        mine = jnp.sum(jnp.where(owner_ref[...] == own, 1, 0), axis=1, keepdims=True)
        owned = mine > s

        @pl.loop(0, width // 256)
        def _(n):
            cols = tile_cols(n, 256)
            moment = mm(rows[0:hid, :], spun[s, :, cols])
            new[s, :, cols] = jnp.where(owned, moment, mom[s, 0:hid, cols].astype(F32)).astype(BF)

        pltpu.make_async_copy(new.at[s], new_hbm.at[s], new_sem.at[s]).start()

    def orthogonalize(s):
        def start(q, total):
            pair = jnp.concatenate(
                [v_buf[s, pl.ds((2 * q + i) * nf, nf)].reshape(upper, 128) for i in range(2)], axis=1
            )
            both = mm(pair, swap[...])
            cols = tile_cols(q, 128)
            for h in range(2):
                part = slice(h * upper, (h + 1) * upper)
                grad = both[:, 128 * h : 128 * h + 128]
                moment = (0.95 * spun[s, part, cols].astype(F32) + grad).astype(BF)
                spun[s, part, cols] = moment
                value = grad + 0.95 * moment.astype(F32)
                nest[part, cols] = value
                total = total + jnp.sum(value * value, axis=0, keepdims=True)
            return total

        total = lax.fori_loop(0, width // 128, start, jnp.zeros((1, 128), F32), unroll=2)
        scale = 1.0 / (jnp.sqrt(jnp.sum(total, axis=1, keepdims=True)) + 1e-07)

        @pl.loop(0, width // 256)
        def _(n):
            cols = tile_cols(n, 256)
            x[:, cols] = (nest[:, cols] * scale).astype(BF)

        @pl.loop(0, ITERS)
        def _(turn):
            for n in range(pad // 256):
                cols = slice(256 * n, 256 * n + 256)
                gram[:, cols] = mm(x[...], x[cols, :], ((1,), (1,))).astype(BF)

            for n in range(pad // 256):
                cols = slice(256 * n, 256 * n + 256)
                part = gram[:, cols]
                square = mm(gram[...], part)
                mixed[:, cols] = (-4.775 * part.astype(F32) + 2.0315 * square).astype(BF)

            for n in range(width // 256):
                cols = slice(256 * n, 256 * n + 256)
                part = x[:, cols]
                product = mm(mixed[...], part)
                x[:, cols] = (3.4445 * part.astype(F32) + product).astype(BF)

        factor = 0.2 * max(hid, width) ** 0.5

        @pl.loop(0, nr // 2, unroll=2)
        def _(q):
            cols = tile_cols(q, 128)
            both = jnp.concatenate(
                [(factor * x[h * upper : (h + 1) * upper, cols].astype(F32)).astype(BF) for h in range(2)], axis=1
            )
            out = mm(both, swap[...])
            for i in range(2):
                w_buf[s, pl.ds((2 * q + i) * nf, nf)] = (
                    out[:, 128 * i : 128 * i + 128].reshape(nf, blk, 128).astype(BF)
                )

    def ungroup(s):
        @pl.loop(0, nf // 2)
        def _(k):
            pair = jnp.concatenate(
                [u_buf[s, pl.ds((2 * k + i) * nr, nr)].reshape(nr * blk, 128) for i in range(2)], axis=1
            )
            out = mm(regroup_t[...], pair).astype(BF)
            s_buf[s, 2 * k] = out[:, :128].reshape(half, nr, 128)
            s_buf[s, 2 * k + 1] = out[:, 128:].reshape(half, nr, 128)

    def along_z(src, dst, send_sem, recv_sem):
        pltpu.make_async_copy(src.at[z], dst.at[z], recv_sem).start()

        @pl.loop(1, nz)
        def _(k):
            to_z = lax.rem(z + k, nz)
            pltpu.make_async_remote_copy(
                src.at[to_z], dst.at[z], send_sem, recv_sem,
                device_id=(rep, 2 * to_z + core), device_id_type=MESH,
            ).start()

    def in_plane(visit):
        @pl.loop(1, 2 * nr)
        def _(k):
            to = lax.rem(2 * rep + core + k, 2 * nr)
            visit(to, to // 2, 2 * z + lax.rem(to, 2))

    def relay_in():
        @pl.loop(0, nz // 2)
        def _(k):
            pair = jnp.concatenate([zr_buf[2 * k + i].reshape(half * nr, 128) for i in range(2)], axis=1)
            out = mm(spread_in[...], pair)
            for i in range(2):
                zt_buf[:, 2 * k + i] = out[:, 128 * i : 128 * i + 128].reshape(2 * nr, blk, 128).astype(BF)

        def send(to, to_r, to_f):
            pltpu.make_async_remote_copy(
                zt_buf.at[to], v_buf.at[1, pl.ds(rep * nf + core * nz, nz)], p_send, in_recv.at[1],
                device_id=(to_r, to_f), device_id_type=MESH,
            ).start()

        pltpu.make_async_copy(
            zt_buf.at[2 * rep + core], v_buf.at[1, pl.ds(rep * nf + core * nz, nz)], in_recv.at[1]
        ).start()
        in_plane(send)

    def plane_out():
        def send(to, to_r, to_f):
            pltpu.make_async_remote_copy(
                w_buf.at[1, pl.ds(to * nz, nz)], zv_buf.at[2 * rep + core], po_send, po_recv,
                device_id=(to_r, to_f), device_id_type=MESH,
            ).start()

        pltpu.make_async_copy(w_buf.at[1, pl.ds((2 * rep + core) * nz, nz)], zv_buf.at[2 * rep + core], po_recv).start()
        in_plane(send)

    def relay_out():
        @pl.loop(0, nz // 2)
        def _(k):
            pair = jnp.concatenate(
                [zv_buf[:, 2 * k + i].reshape(2 * nr * blk, 128) for i in range(2)], axis=1
            )
            out = mm(spread_out[...], pair).astype(BF)
            for i in range(2):
                zs_buf[2 * k + i] = out[:, 128 * i : 128 * i + 128].reshape(half, nr, 128)

    def unpack(second):
        chosen = [select(0), select(1)]

        @pl.loop(0, half)
        def _(a):
            first = mm(s_buf[0, :, a].reshape(mats, 128), chosen[0], ((0,), (0,)))
            out = (first + mm(second(a), chosen[1], ((0,), (0,)))).astype(BF)
            upd_ref[a] = out[0:64]
            upd_ref[a + half] = out[64:128]

    def all_but_one(ref):
        return ref.at[pl.ds(0, ref.shape[0] - 1)]

    loads[0].wait()
    if relayed:
        gather(1)
        pl.semaphore_wait(barrier, mats - 1)
        along_z(zs_buf, zr_buf, z_send, z_recv)
        gather(0)
        for load in loads[1:]:
            load.wait()

        @pl.loop(0, nf // 2)
        def _(k):
            regroup_two(0, 2 * k)

        spin_momentum(1)
        spin_momentum(0)

        wait_bytes(zr_buf, z_recv)
        relay_in()
        send_in(0, True)
        wait_bytes(v_buf.at[1], in_recv.at[1])
        orthogonalize(1)
        plane_out()

        wait_bytes(v_buf.at[0], in_recv.at[0])
        orthogonalize(0)
        send_out(0)

        wait_bytes(zv_buf, po_recv)
        wait_bytes(all_but_one(zs_buf), z_send)
        relay_out()
        along_z(zs_buf, zu_buf, zo_send, zo_recv)
        store_momentum(1)
        store_momentum(0)

        wait_bytes(u_buf.at[0], out_recv.at[0])
        ungroup(0)
        wait_bytes(zu_buf, zo_recv)
        unpack(lambda a: zu_buf[:, a].reshape(nz * nr, 128))
        wait_bytes(all_but_one(zt_buf), p_send)
        wait_bytes(all_but_one(zv_buf), po_send)
        wait_bytes(all_but_one(zs_buf), zo_send)
    else:
        gather(0)
        for load in loads[1:]:
            load.wait()
        pl.semaphore_wait(barrier, mats - 1)
        send_in(0, False)
        gather(1)
        send_in(1, False)
        spin_momentum(0)
        spin_momentum(1)
        for s in range(2):
            wait_bytes(v_buf.at[s], in_recv.at[s])
            orthogonalize(s)
            send_out(s)
        for s in range(2):
            store_momentum(s)
        for s in range(2):
            wait_bytes(u_buf.at[s], out_recv.at[s])
            ungroup(s)
        unpack(lambda a: s_buf[1, :, a].reshape(mats, 128))

    for s in range(2):
        wait_bytes(new.at[s], new_sem.at[s])
    for s in range(1 if relayed else 2):
        wait_bytes(all_but_one(t_buf.at[s]), in_send.at[s])
        wait_bytes(all_but_one(w_buf.at[s]), out_send.at[s])


def one_hot(rows, cols, pairs):
    out = np.zeros((rows, cols), np.float32)
    for i, j in pairs:
        out[i, j] = 1.0
    return jnp.asarray(out, BF)


def on_device(grads, momentum, owner):
    nf, nr = lax.axis_size("fsdp"), lax.axis_size("rep")
    mats, tile_rows, tile_cols = grads.shape
    half = tile_rows // 2
    hid, width = nf * tile_rows, nr * tile_cols
    blk = half + 2
    upper = nf * blk
    pad = 2 * upper
    nz = nf // 2

    regroup_pairs = [(r * blk + a, a * nr + r) for r in range(nr) for a in range(half)]
    row_pairs = [
        (tile_rows * f + half * h + a, h * upper + (f % 2 * nz + f // 2) * blk + a)
        for f in range(nf) for h in range(2) for a in range(half)
    ]
    swap_pairs = [(i * 128 + j * 64 + c, j * 128 + i * 64 + c) for i in range(2) for j in range(2) for c in range(64)]
    flip = lambda pairs: [(j, i) for i, j in pairs]
    regroup = one_hot(nr * blk, half * nr, regroup_pairs)
    regroup_t = one_hot(half * nr, nr * blk, flip(regroup_pairs))
    rows = one_hot(pad, pad, row_pairs)
    rows_t = one_hot(pad, pad, flip(row_pairs))
    swap = one_hot(256, 256, swap_pairs)

    vmem = pl.BlockSpec(memory_space=pltpu.VMEM)
    hbm = pl.BlockSpec(memory_space=pl.ANY)
    cfg = (nr, nf, half, hid, width, pad)
    turned = grads.transpose(1, 2, 0)
    tables = [regroup, regroup_t, rows, rows_t, swap]
    by_f = pltpu.VMEM((2, nf, half, nr, 128), BF)
    tiles = pltpu.VMEM((2, mats, blk, 128), BF)
    by_z = pltpu.VMEM((nz, half, nr, 128), BF)
    in_plane = pltpu.VMEM((2 * nr, nz, blk, 128), BF)
    one = pltpu.SemaphoreType.DMA(())
    relay_scratch = [
        by_z, by_z, in_plane, in_plane, by_z,
        pltpu.VMEM((2 * nr * blk, half * nr), BF),
        pltpu.VMEM((half * nr, 2 * nr * blk), BF),
        *[one for _ in range(7)],
    ]

    def run(relayed, operands):
        return pl.pallas_call(
            functools.partial(kernel, cfg, relayed),
            out_shape=(
                jax.ShapeDtypeStruct((tile_rows, tile_cols, mats), BF),
                jax.ShapeDtypeStruct(momentum.shape[1:], BF),
            ),
            in_specs=[vmem] + [hbm] * 7,
            out_specs=(vmem, hbm),
            scratch_shapes=[
                pltpu.VMEM(turned.shape, BF),
                *[pltpu.VMEM(table.shape, BF) for table in tables],
                pltpu.VMEM((2, mats), jnp.int32),
                by_f, tiles, tiles, tiles, tiles,
                pltpu.VMEM((2, pad, width), BF),
                pltpu.VMEM((2, pad, width), BF),
                pltpu.VMEM((2, hid, width), BF),
                pltpu.VMEM((pad, width), F32),
                pltpu.VMEM((pad, width), BF),
                pltpu.VMEM((pad, pad), BF),
                pltpu.VMEM((pad, pad), BF),
                pltpu.SemaphoreType.DMA((6,)),
                *[pltpu.SemaphoreType.DMA((2,)) for _ in range(6)],
                *(relay_scratch if relayed else []),
            ],
            compiler_params=pltpu.CompilerParams(
                collective_id=1 if relayed else 0, has_side_effects=True, vmem_limit_bytes=58 * 1024 * 1024
            ),
            name="muon_relayed" if relayed else "muon_direct",
        )(*operands)

    order = jnp.arange(mats, dtype=jnp.int32)
    second = (owner[:, None] == owner[None, :]) & (order[:, None] < order[None, :])
    plane = (owner % nf) // 2
    in_each = second[None] & (plane[None, None, :] == jnp.arange(nz, dtype=jnp.int32)[:, None, None])
    fits = jnp.max(jnp.sum(in_each.astype(jnp.int32), axis=(1, 2))) <= nr
    operands = (owner[None, :], turned, momentum[0], *tables)
    update, new = lax.cond(fits, functools.partial(run, True), functools.partial(run, False), operands)
    return (update.transpose(2, 0, 1), new[None])


def solution(mesh):
    return jax.shard_map(
        on_device,
        mesh=mesh,
        in_specs=(P(None, "fsdp", "rep"), P(("rep", "fsdp"), None, None, None), P()),
        out_specs=(P(None, "fsdp", "rep"), P(("rep", "fsdp"), None, None, None)),
        check_vma=False,
    )
```

```python
import functools

import jax
import jax.numpy as jnp
import numpy as np
from jax import lax
from jax.experimental import pallas as pl
from jax.experimental.pallas import tpu as pltpu
from jax.sharding import PartitionSpec as P

ITERS = 2
MESH = pl.DeviceIdType.MESH
BF = jnp.bfloat16
F32 = jnp.float32


def mm(a, b, dims=((1,), (0,))):
    return lax.dot_general(a, b, (dims, ((), ())), preferred_element_type=F32)


def wait_bytes(ref, sem):
    pltpu.make_async_copy(ref, ref, sem).wait()


def tile_cols(n, size):
    return pl.ds(pl.multiple_of(n * size, size), size)


def kernel(
    cfg, relayed,
    owner_ref, g_hbm, mom_hbm, regroup_hbm, regroup_t_hbm, rows_hbm, rows_t_hbm, swap_hbm,
    upd_ref, new_hbm,
    g, regroup, regroup_t, rows, rows_t, swap, keys,
    s_buf, t_buf, v_buf, w_buf, u_buf, mom, spun, new, nest, x, gram, mixed,
    load_sem, mom_sem, new_sem, in_send, in_recv, out_send, out_recv,
    *relay_refs,
):
    nr, nf, half, hid, width, pad = cfg
    rep, fs = lax.axis_index("rep"), lax.axis_index("fsdp")
    mats = nr * nf
    blk = half + 2
    upper = nf * blk
    nz = nf // 2
    z, core = fs // 2, lax.rem(fs, 2)
    lane = rep * nf + core * nz + z
    if relayed:
        (zs_buf, zr_buf, zt_buf, zv_buf, zu_buf, spread_in, spread_out,
         z_send, z_recv, p_send, zo_send, zo_recv, po_send, po_recv) = relay_refs

    loads = [(g_hbm, g), (regroup_hbm, regroup), (swap_hbm, swap), (rows_hbm, rows),
             (rows_t_hbm, rows_t), (regroup_t_hbm, regroup_t)]
    loads = [pltpu.make_async_copy(a, b, load_sem.at[i]) for i, (a, b) in enumerate(loads)]
    for load in loads:
        load.start()
    for s in range(2):
        pltpu.make_async_copy(mom_hbm.at[s], mom.at[s, pl.ds(0, hid)], mom_sem.at[s]).start()

    side = 4
    rx, ry = rep // side, lax.rem(rep, side)

    def moved(j):
        return lax.rem(rx + j, side) * side + lax.rem(ry + j // side + j, side)

    def faces(dz, dc):
        return 2 * lax.rem(z + dz, nz) + lax.rem(core + dc, 2)

    def everyone(visit):
        @pl.loop(0, nz // 2 - 1)
        def _(k):
            @pl.loop(0, nr)
            def _(j):
                to_r = moved(j)
                for dc in range(2):
                    visit(to_r, faces(k + 1, dc))
                    visit(to_r, faces(nz - 1 - k, dc))

        for dc in range(2):
            visit(rep, faces(nz // 2, dc))
        visit(rep, faces(0, 1))

        @pl.loop(1, nr)
        def _(j):
            to_r = moved(j)
            for dc in range(2):
                visit(to_r, faces(nz // 2, dc))
                visit(to_r, faces(0, dc))

    barrier = pltpu.get_barrier_semaphore()

    def greet(to_r, to_f):
        pl.semaphore_signal(barrier, inc=1, device_id=(to_r, to_f), device_id_type=MESH)

    everyone(greet)

    owner = owner_ref[...]
    down = jnp.transpose(jnp.broadcast_to(owner, (mats, mats)))
    index = lax.broadcasted_iota(jnp.int32, (mats, mats), 0)
    order = lax.broadcasted_iota(jnp.int32, (mats, mats), 1)
    earlier = (down == owner) & (index < order)
    slot = jnp.sum(jnp.where(earlier, 1, 0), axis=0, keepdims=True)
    place = (owner % nf) * nr + owner // nf
    keys[0:1, :] = jnp.where(slot == 0, place, -1)
    if relayed:
        plane = jnp.where(slot == 1, (owner % nf) // 2, -1)
        plane_down = jnp.transpose(jnp.broadcast_to(plane, (mats, mats)))
        before = (plane_down == plane) & (index < order)
        rank = jnp.sum(jnp.where(before, 1, 0), axis=0, keepdims=True)
        keys[1:2, :] = jnp.where(slot == 1, plane * nr + rank, -1)
        member = (owner // nf) * 2 + owner % 2 + 1
        wide = half * nr
        column = lax.broadcasted_iota(jnp.int32, (wide, mats), 0) % nr
        here = jnp.where(keys[1:2, :] == z * nr + column, 1.0, 0.0).astype(BF)
        members = jnp.broadcast_to(member, (8, mats)).astype(F32).astype(BF)
        owner_of = mm(members, here, ((1,), (1,)))[0:1, :]
        line = lax.broadcasted_iota(jnp.int32, (2 * nr * blk, wide), 0)
        source = lax.broadcasted_iota(jnp.int32, (2 * nr * blk, wide), 1)
        wanted = (owner_of == (line // blk + 1).astype(F32)) & (line % blk == source // nr)
        wanted = jnp.where(wanted, 1.0, 0.0)
        spread_in[...] = wanted.astype(BF)
        spread_out[...] = jnp.transpose(wanted).astype(BF)
    else:
        keys[1:2, :] = jnp.where(slot == 1, place, -1)

    def select(s):
        places = nz * nr if relayed and s == 1 else mats
        slot_id = lax.broadcasted_iota(jnp.int32, (places, mats), 0)
        return jnp.where(slot_id == keys[s : s + 1, :], 1.0, 0.0).astype(BF)

    def gather(s):
        chosen = select(s)

        @pl.loop(0, half)
        def _(a):
            both = jnp.concatenate([g[a], g[a + half]], axis=0)
            out = mm(chosen, both, ((1,), (1,))).astype(BF)
            if relayed and s == 1:
                zs_buf[:, a] = out.reshape(nz, nr, 128)
            else:
                s_buf[s, :, a] = out.reshape(nf, nr, 128)

    def regroup_two(s, k):
        first, second = k, k + 1
        pair = jnp.concatenate(
            [s_buf[s, first].reshape(half * nr, 128), s_buf[s, second].reshape(half * nr, 128)], axis=1
        )
        out = mm(regroup[...], pair)
        t_buf[s, pl.ds(first * nr, nr)] = out[:, :128].reshape(nr, blk, 128).astype(BF)
        t_buf[s, pl.ds(second * nr, nr)] = out[:, 128:].reshape(nr, blk, 128).astype(BF)

    def regroup_all(s):
        @pl.loop(0, nf // 2)
        def _(k):
            regroup_two(s, 2 * k)

    def send_in(s, regrouped):
        def send(to_r, to_f):
            pltpu.make_async_remote_copy(
                t_buf.at[s, to_f * nr + to_r], v_buf.at[s, lane], in_send.at[s], in_recv.at[s],
                device_id=(to_r, to_f), device_id_type=MESH,
            ).start()

        if not regrouped:
            regroup_all(s)
        pltpu.make_async_copy(t_buf.at[s, fs * nr + rep], v_buf.at[s, lane], in_recv.at[s]).start()
        everyone(send)

    def send_out(s):
        def send(to_r, to_f):
            pltpu.make_async_remote_copy(
                w_buf.at[s, to_r * nf + lax.rem(to_f, 2) * nz + to_f // 2], u_buf.at[s, fs * nr + rep], out_send.at[s], out_recv.at[s],
                device_id=(to_r, to_f), device_id_type=MESH,
            ).start()

        pltpu.make_async_copy(w_buf.at[s, lane], u_buf.at[s, fs * nr + rep], out_recv.at[s]).start()
        everyone(send)

    def spin_momentum(s):
        wait_bytes(mom.at[s, pl.ds(0, hid)], mom_sem.at[s])
        if pad > hid:
            mom[s, hid:pad, :] = jnp.zeros((pad - hid, width), BF)

        @pl.loop(0, width // 256)
        def _(n):
            cols = tile_cols(n, 256)
            spun[s, :, cols] = mm(rows_t[...], mom[s, :, cols]).astype(BF)

    def store_momentum(s):
        own = rep * nf + fs
        mine = jnp.sum(jnp.where(owner_ref[...] == own, 1, 0), axis=1, keepdims=True)
        owned = mine > s

        @pl.loop(0, width // 256)
        def _(n):
            cols = tile_cols(n, 256)
            moment = mm(rows[0:hid, :], spun[s, :, cols])
            new[s, :, cols] = jnp.where(owned, moment, mom[s, 0:hid, cols].astype(F32)).astype(BF)

        pltpu.make_async_copy(new.at[s], new_hbm.at[s], new_sem.at[s]).start()

    def orthogonalize(s):
        def start(q, total):
            pair = jnp.concatenate(
                [v_buf[s, pl.ds((2 * q + i) * nf, nf)].reshape(upper, 128) for i in range(2)], axis=1
            )
            both = mm(pair, swap[...])
            cols = tile_cols(q, 128)
            for h in range(2):
                part = slice(h * upper, (h + 1) * upper)
                grad = both[:, 128 * h : 128 * h + 128]
                moment = (0.95 * spun[s, part, cols].astype(F32) + grad).astype(BF)
                spun[s, part, cols] = moment
                value = grad + 0.95 * moment.astype(F32)
                nest[part, cols] = value
                total = total + jnp.sum(value * value, axis=0, keepdims=True)
            return total

        total = lax.fori_loop(0, width // 128, start, jnp.zeros((1, 128), F32), unroll=2)
        scale = 1.0 / (jnp.sqrt(jnp.sum(total, axis=1, keepdims=True)) + 1e-07)

        @pl.loop(0, width // 256)
        def _(n):
            cols = tile_cols(n, 256)
            x[:, cols] = (nest[:, cols] * scale).astype(BF)

        @pl.loop(0, ITERS)
        def _(turn):
            for n in range(pad // 256):
                cols = slice(256 * n, 256 * n + 256)
                gram[:, cols] = mm(x[...], x[cols, :], ((1,), (1,))).astype(BF)

            for n in range(pad // 256):
                cols = slice(256 * n, 256 * n + 256)
                part = gram[:, cols]
                square = mm(gram[...], part)
                mixed[:, cols] = (-4.775 * part.astype(F32) + 2.0315 * square).astype(BF)

            for n in range(width // 256):
                cols = slice(256 * n, 256 * n + 256)
                part = x[:, cols]
                product = mm(mixed[...], part)
                x[:, cols] = (3.4445 * part.astype(F32) + product).astype(BF)

        factor = 0.2 * max(hid, width) ** 0.5

        @pl.loop(0, nr // 2, unroll=2)
        def _(q):
            cols = tile_cols(q, 128)
            both = jnp.concatenate(
                [(factor * x[h * upper : (h + 1) * upper, cols].astype(F32)).astype(BF) for h in range(2)], axis=1
            )
            out = mm(both, swap[...])
            for i in range(2):
                w_buf[s, pl.ds((2 * q + i) * nf, nf)] = (
                    out[:, 128 * i : 128 * i + 128].reshape(nf, blk, 128).astype(BF)
                )

    def ungroup(s):
        @pl.loop(0, nf // 2)
        def _(k):
            pair = jnp.concatenate(
                [u_buf[s, pl.ds((2 * k + i) * nr, nr)].reshape(nr * blk, 128) for i in range(2)], axis=1
            )
            out = mm(regroup_t[...], pair).astype(BF)
            s_buf[s, 2 * k] = out[:, :128].reshape(half, nr, 128)
            s_buf[s, 2 * k + 1] = out[:, 128:].reshape(half, nr, 128)

    def along_z(src, dst, send_sem, recv_sem):
        pltpu.make_async_copy(src.at[z], dst.at[z], recv_sem).start()

        def send(dz):
            to_z = lax.rem(z + dz, nz)
            pltpu.make_async_remote_copy(
                src.at[to_z], dst.at[z], send_sem, recv_sem,
                device_id=(rep, 2 * to_z + core), device_id_type=MESH,
            ).start()

        send(nz // 2)
        for k in range(nz // 2 - 1, 0, -1):
            send(k)
            send(nz - k)

    def in_plane(visit):
        visit(2 * rep + 1 - core, rep, 2 * z + 1 - core)

        @pl.loop(1, nr)
        def _(j):
            to_r = moved(j)
            for dc in range(2):
                to_c = lax.rem(core + dc, 2)
                visit(2 * to_r + to_c, to_r, 2 * z + to_c)

    def relay_in():
        @pl.loop(0, nz // 2)
        def _(k):
            pair = jnp.concatenate([zr_buf[2 * k + i].reshape(half * nr, 128) for i in range(2)], axis=1)
            out = mm(spread_in[...], pair)
            for i in range(2):
                zt_buf[:, 2 * k + i] = out[:, 128 * i : 128 * i + 128].reshape(2 * nr, blk, 128).astype(BF)

        def send(to, to_r, to_f):
            pltpu.make_async_remote_copy(
                zt_buf.at[to], v_buf.at[1, pl.ds(rep * nf + core * nz, nz)], p_send, in_recv.at[1],
                device_id=(to_r, to_f), device_id_type=MESH,
            ).start()

        pltpu.make_async_copy(
            zt_buf.at[2 * rep + core], v_buf.at[1, pl.ds(rep * nf + core * nz, nz)], in_recv.at[1]
        ).start()
        in_plane(send)

    def plane_out():
        def send(to, to_r, to_f):
            pltpu.make_async_remote_copy(
                w_buf.at[1, pl.ds(to * nz, nz)], zv_buf.at[2 * rep + core], po_send, po_recv,
                device_id=(to_r, to_f), device_id_type=MESH,
            ).start()

        pltpu.make_async_copy(w_buf.at[1, pl.ds((2 * rep + core) * nz, nz)], zv_buf.at[2 * rep + core], po_recv).start()
        in_plane(send)

    def relay_out():
        @pl.loop(0, nz // 2)
        def _(k):
            pair = jnp.concatenate(
                [zv_buf[:, 2 * k + i].reshape(2 * nr * blk, 128) for i in range(2)], axis=1
            )
            out = mm(spread_out[...], pair).astype(BF)
            for i in range(2):
                zs_buf[2 * k + i] = out[:, 128 * i : 128 * i + 128].reshape(half, nr, 128)

    def unpack(second):
        chosen = [select(0), select(1)]

        @pl.loop(0, half)
        def _(a):
            first = mm(s_buf[0, :, a].reshape(mats, 128), chosen[0], ((0,), (0,)))
            out = (first + mm(second(a), chosen[1], ((0,), (0,)))).astype(BF)
            upd_ref[a] = out[0:64]
            upd_ref[a + half] = out[64:128]

    def all_but_one(ref):
        return ref.at[pl.ds(0, ref.shape[0] - 1)]

    loads[0].wait()
    if relayed:
        gather(1)
        pl.semaphore_wait(barrier, mats - 1)
        along_z(zs_buf, zr_buf, z_send, z_recv)
        gather(0)
        for load in loads[1:]:
            load.wait()
        regroup_all(0)
        spin_momentum(1)
        spin_momentum(0)

        wait_bytes(zr_buf, z_recv)
        relay_in()
        send_in(0, True)
        wait_bytes(v_buf.at[1], in_recv.at[1])
        orthogonalize(1)
        plane_out()

        wait_bytes(v_buf.at[0], in_recv.at[0])
        orthogonalize(0)
        send_out(0)

        wait_bytes(zv_buf, po_recv)
        wait_bytes(all_but_one(zs_buf), z_send)
        relay_out()
        along_z(zs_buf, zu_buf, zo_send, zo_recv)
        store_momentum(1)
        store_momentum(0)

        wait_bytes(u_buf.at[0], out_recv.at[0])
        ungroup(0)
        wait_bytes(zu_buf, zo_recv)
        unpack(lambda a: zu_buf[:, a].reshape(nz * nr, 128))
        wait_bytes(all_but_one(zt_buf), p_send)
        wait_bytes(all_but_one(zv_buf), po_send)
        wait_bytes(all_but_one(zs_buf), zo_send)
    else:
        gather(0)
        for load in loads[1:]:
            load.wait()
        pl.semaphore_wait(barrier, mats - 1)
        send_in(0, False)
        gather(1)
        send_in(1, False)
        spin_momentum(0)
        spin_momentum(1)
        for s in range(2):
            wait_bytes(v_buf.at[s], in_recv.at[s])
            orthogonalize(s)
            send_out(s)
        for s in range(2):
            store_momentum(s)
        for s in range(2):
            wait_bytes(u_buf.at[s], out_recv.at[s])
            ungroup(s)
        unpack(lambda a: s_buf[1, :, a].reshape(mats, 128))

    for s in range(2):
        wait_bytes(new.at[s], new_sem.at[s])
    for s in range(1 if relayed else 2):
        wait_bytes(all_but_one(t_buf.at[s]), in_send.at[s])
        wait_bytes(all_but_one(w_buf.at[s]), out_send.at[s])


def one_hot(rows, cols, pairs):
    out = np.zeros((rows, cols), np.float32)
    for i, j in pairs:
        out[i, j] = 1.0
    return jnp.asarray(out, BF)


def on_device(grads, momentum, owner):
    nf, nr = lax.axis_size("fsdp"), lax.axis_size("rep")
    mats, tile_rows, tile_cols = grads.shape
    half = tile_rows // 2
    hid, width = nf * tile_rows, nr * tile_cols
    blk = half + 2
    upper = nf * blk
    pad = 2 * upper
    nz = nf // 2

    regroup_pairs = [(r * blk + a, a * nr + r) for r in range(nr) for a in range(half)]
    row_pairs = [
        (tile_rows * f + half * h + a, h * upper + (f % 2 * nz + f // 2) * blk + a)
        for f in range(nf) for h in range(2) for a in range(half)
    ]
    swap_pairs = [(i * 128 + j * 64 + c, j * 128 + i * 64 + c) for i in range(2) for j in range(2) for c in range(64)]
    flip = lambda pairs: [(j, i) for i, j in pairs]
    regroup = one_hot(nr * blk, half * nr, regroup_pairs)
    regroup_t = one_hot(half * nr, nr * blk, flip(regroup_pairs))
    rows = one_hot(pad, pad, row_pairs)
    rows_t = one_hot(pad, pad, flip(row_pairs))
    swap = one_hot(256, 256, swap_pairs)

    vmem = pl.BlockSpec(memory_space=pltpu.VMEM)
    hbm = pl.BlockSpec(memory_space=pl.ANY)
    cfg = (nr, nf, half, hid, width, pad)
    turned = grads.transpose(1, 2, 0)
    tables = [regroup, regroup_t, rows, rows_t, swap]
    by_f = pltpu.VMEM((2, nf, half, nr, 128), BF)
    tiles = pltpu.VMEM((2, mats, blk, 128), BF)
    by_z = pltpu.VMEM((nz, half, nr, 128), BF)
    in_plane = pltpu.VMEM((2 * nr, nz, blk, 128), BF)
    one = pltpu.SemaphoreType.DMA(())
    relay_scratch = [
        by_z, by_z, in_plane, in_plane, by_z,
        pltpu.VMEM((2 * nr * blk, half * nr), BF),
        pltpu.VMEM((half * nr, 2 * nr * blk), BF),
        *[one for _ in range(7)],
    ]

    def run(relayed, operands):
        return pl.pallas_call(
            functools.partial(kernel, cfg, relayed),
            out_shape=(
                jax.ShapeDtypeStruct((tile_rows, tile_cols, mats), BF),
                jax.ShapeDtypeStruct(momentum.shape[1:], BF),
            ),
            in_specs=[vmem] + [hbm] * 7,
            out_specs=(vmem, hbm),
            scratch_shapes=[
                pltpu.VMEM(turned.shape, BF),
                *[pltpu.VMEM(table.shape, BF) for table in tables],
                pltpu.VMEM((2, mats), jnp.int32),
                by_f, tiles, tiles, tiles, tiles,
                pltpu.VMEM((2, pad, width), BF),
                pltpu.VMEM((2, pad, width), BF),
                pltpu.VMEM((2, hid, width), BF),
                pltpu.VMEM((pad, width), F32),
                pltpu.VMEM((pad, width), BF),
                pltpu.VMEM((pad, pad), BF),
                pltpu.VMEM((pad, pad), BF),
                pltpu.SemaphoreType.DMA((6,)),
                *[pltpu.SemaphoreType.DMA((2,)) for _ in range(6)],
                *(relay_scratch if relayed else []),
            ],
            compiler_params=pltpu.CompilerParams(
                collective_id=1 if relayed else 0, has_side_effects=True, vmem_limit_bytes=58 * 1024 * 1024
            ),
            name="muon_relayed" if relayed else "muon_direct",
        )(*operands)

    order = jnp.arange(mats, dtype=jnp.int32)
    second = (owner[:, None] == owner[None, :]) & (order[:, None] < order[None, :])
    plane = (owner % nf) // 2
    in_each = second[None] & (plane[None, None, :] == jnp.arange(nz, dtype=jnp.int32)[:, None, None])
    fits = jnp.max(jnp.sum(in_each.astype(jnp.int32), axis=(1, 2))) <= nr
    operands = (owner[None, :], turned, momentum[0], *tables)
    update, new = lax.cond(fits, functools.partial(run, True), functools.partial(run, False), operands)
    return (update.transpose(2, 0, 1), new[None])


def solution(mesh):
    return jax.shard_map(
        on_device,
        mesh=mesh,
        in_specs=(P(None, "fsdp", "rep"), P(("rep", "fsdp"), None, None, None), P()),
        out_specs=(P(None, "fsdp", "rep"), P(("rep", "fsdp"), None, None, None)),
        check_vma=False,
    )
```

```python
import functools

import jax
import jax.numpy as jnp
import numpy as np
from jax import lax
from jax.experimental import pallas as pl
from jax.experimental.pallas import tpu as pltpu
from jax.sharding import PartitionSpec as P

ITERS = 2
MESH = pl.DeviceIdType.MESH
BF = jnp.bfloat16
F32 = jnp.float32


def mm(a, b, dims=((1,), (0,))):
    return lax.dot_general(a, b, (dims, ((), ())), preferred_element_type=F32)


def wait_bytes(ref, sem):
    pltpu.make_async_copy(ref, ref, sem).wait()


def tile_cols(n, size):
    return pl.ds(pl.multiple_of(n * size, size), size)


def kernel(
    cfg, relayed,
    owner_ref, g_hbm, mom_hbm, regroup_hbm, regroup_t_hbm, rows_hbm, rows_t_hbm, swap_hbm,
    upd_ref, new_hbm,
    g, regroup, regroup_t, rows, rows_t, swap, keys,
    s_buf, t_buf, v_buf, w_buf, u_buf, mom, spun, new, nest, x, gram, mixed,
    load_sem, mom_sem, new_sem, in_send, in_recv, out_send, out_recv,
    *relay_refs,
):
    nr, nf, half, hid, width, pad = cfg
    rep, fs = lax.axis_index("rep"), lax.axis_index("fsdp")
    mats = nr * nf
    blk = half + 2
    upper = nf * blk
    nz = nf // 2
    z, core = fs // 2, lax.rem(fs, 2)
    lane = rep * nf + core * nz + z
    if relayed:
        (zs_buf, zr_buf, zt_buf, zv_buf, zu_buf, spread_in, spread_out,
         z_send, z_recv, p_send, zo_send, zo_recv, po_send, po_recv) = relay_refs

    loads = [(g_hbm, g), (regroup_hbm, regroup), (swap_hbm, swap), (rows_hbm, rows),
             (rows_t_hbm, rows_t), (regroup_t_hbm, regroup_t)]
    loads = [pltpu.make_async_copy(a, b, load_sem.at[i]) for i, (a, b) in enumerate(loads)]
    for load in loads:
        load.start()
    for s in range(2):
        pltpu.make_async_copy(mom_hbm.at[s], mom.at[s, pl.ds(0, hid)], mom_sem.at[s]).start()

    side = 4
    rx, ry = rep // side, lax.rem(rep, side)

    def moved(j):
        return lax.rem(rx + j, side) * side + lax.rem(ry + j // side + j, side)

    def faces(dz, dc):
        return 2 * lax.rem(z + dz, nz) + lax.rem(core + dc, 2)

    def everyone(visit):
        @pl.loop(0, nz // 2 - 1)
        def _(k):
            @pl.loop(0, nr)
            def _(j):
                to_r = moved(j)
                for dc in range(2):
                    visit(to_r, faces(k + 1, dc))
                    visit(to_r, faces(nz - 1 - k, dc))

        for dc in range(2):
            visit(rep, faces(nz // 2, dc))
        visit(rep, faces(0, 1))

        @pl.loop(1, nr)
        def _(j):
            to_r = moved(j)
            for dc in range(2):
                visit(to_r, faces(nz // 2, dc))
                visit(to_r, faces(0, dc))

    barrier = pltpu.get_barrier_semaphore()

    def greet(t):
        to_r = lax.rem(rx + t, side) * side + lax.rem(ry + t // side, side)
        to_f = lax.rem(fs + t // nr, nf)
        pl.semaphore_signal(barrier, inc=1, device_id=(to_r, to_f), device_id_type=MESH)

    owner = owner_ref[...]
    down = jnp.transpose(jnp.broadcast_to(owner, (mats, mats)))
    index = lax.broadcasted_iota(jnp.int32, (mats, mats), 0)
    order = lax.broadcasted_iota(jnp.int32, (mats, mats), 1)
    earlier = (down == owner) & (index < order)
    slot = jnp.sum(jnp.where(earlier, 1, 0), axis=0, keepdims=True)
    place = (owner % nf) * nr + owner // nf
    keys[0:1, :] = jnp.where(slot == 0, place, -1)
    if relayed:
        plane = jnp.where(slot == 1, (owner % nf) // 2, -1)
        plane_down = jnp.transpose(jnp.broadcast_to(plane, (mats, mats)))
        before = (plane_down == plane) & (index < order)
        rank = jnp.sum(jnp.where(before, 1, 0), axis=0, keepdims=True)
        keys[1:2, :] = jnp.where(slot == 1, plane * nr + rank, -1)
    else:
        keys[1:2, :] = jnp.where(slot == 1, place, -1)

    def relay_matrices():
        member = (owner // nf) * 2 + owner % 2 + 1
        wide = half * nr
        column = lax.broadcasted_iota(jnp.int32, (wide, mats), 0) % nr
        here = jnp.where(keys[1:2, :] == z * nr + column, 1.0, 0.0).astype(BF)
        members = jnp.broadcast_to(member, (8, mats)).astype(F32).astype(BF)
        owner_of = mm(members, here, ((1,), (1,)))[0:1, :]
        line = lax.broadcasted_iota(jnp.int32, (2 * nr * blk, wide), 0)
        source = lax.broadcasted_iota(jnp.int32, (2 * nr * blk, wide), 1)
        wanted = (owner_of == (line // blk + 1).astype(F32)) & (line % blk == source // nr)
        wanted = jnp.where(wanted, 1.0, 0.0)
        spread_in[...] = wanted.astype(BF)
        spread_out[...] = jnp.transpose(wanted).astype(BF)

    def select(s):
        places = nz * nr if relayed and s == 1 else mats
        slot_id = lax.broadcasted_iota(jnp.int32, (places, mats), 0)
        return jnp.where(slot_id == keys[s : s + 1, :], 1.0, 0.0).astype(BF)

    def gather(s, greeting):
        chosen = select(s)
        def one_row(a):
            both = jnp.concatenate([g[a], g[a + half]], axis=0)
            out = mm(chosen, both, ((1,), (1,))).astype(BF)
            if relayed and s == 1:
                zs_buf[:, a] = out.reshape(nz, nr, 128)
            else:
                s_buf[s, :, a] = out.reshape(nf, nr, 128)

        rounds = (mats - 1) // 15

        @pl.loop(0, rounds)
        def _(a):
            if greeting:
                for t in range(15):
                    greet(15 * a + t + 1)
            one_row(a)

        @pl.loop(rounds, half)
        def _(a):
            one_row(a)

    def regroup_two(s, k):
        first, second = k, k + 1
        pair = jnp.concatenate(
            [s_buf[s, first].reshape(half * nr, 128), s_buf[s, second].reshape(half * nr, 128)], axis=1
        )
        out = mm(regroup[...], pair)
        t_buf[s, pl.ds(first * nr, nr)] = out[:, :128].reshape(nr, blk, 128).astype(BF)
        t_buf[s, pl.ds(second * nr, nr)] = out[:, 128:].reshape(nr, blk, 128).astype(BF)

    def regroup_all(s):
        @pl.loop(0, nf // 2)
        def _(k):
            regroup_two(s, 2 * k)

    def send_in(s, regrouped):
        def send(to_r, to_f):
            pltpu.make_async_remote_copy(
                t_buf.at[s, to_f * nr + to_r], v_buf.at[s, lane], in_send.at[s], in_recv.at[s],
                device_id=(to_r, to_f), device_id_type=MESH,
            ).start()

        if not regrouped:
            regroup_all(s)
        pltpu.make_async_copy(t_buf.at[s, fs * nr + rep], v_buf.at[s, lane], in_recv.at[s]).start()
        everyone(send)

    def send_out(s):
        def send(to_r, to_f):
            pltpu.make_async_remote_copy(
                w_buf.at[s, to_r * nf + lax.rem(to_f, 2) * nz + to_f // 2], u_buf.at[s, fs * nr + rep], out_send.at[s], out_recv.at[s, z],
                device_id=(to_r, to_f), device_id_type=MESH,
            ).start()

        pltpu.make_async_copy(w_buf.at[s, lane], u_buf.at[s, fs * nr + rep], out_recv.at[s, z]).start()
        everyone(send)

    def spin_momentum(s):
        wait_bytes(mom.at[s, pl.ds(0, hid)], mom_sem.at[s])
        if pad > hid:
            mom[s, hid:pad, :] = jnp.zeros((pad - hid, width), BF)

        @pl.loop(0, width // 256)
        def _(n):
            cols = tile_cols(n, 256)
            spun[s, :, cols] = mm(rows_t[...], mom[s, :, cols]).astype(BF)

    def store_momentum(s):
        own = rep * nf + fs
        mine = jnp.sum(jnp.where(owner_ref[...] == own, 1, 0), axis=1, keepdims=True)
        owned = mine > s

        @pl.loop(0, width // 256)
        def _(n):
            cols = tile_cols(n, 256)
            moment = mm(rows[0:hid, :], spun[s, :, cols])
            new[s, :, cols] = jnp.where(owned, moment, mom[s, 0:hid, cols].astype(F32)).astype(BF)

        pltpu.make_async_copy(new.at[s], new_hbm.at[s], new_sem.at[s]).start()

    def orthogonalize(s, before_last):
        def start(q, total):
            pair = jnp.concatenate(
                [v_buf[s, pl.ds((2 * q + i) * nf, nf)].reshape(upper, 128) for i in range(2)], axis=1
            )
            both = mm(pair, swap[...])
            cols = tile_cols(q, 128)
            for h in range(2):
                part = slice(h * upper, (h + 1) * upper)
                grad = both[:, 128 * h : 128 * h + 128]
                moment = (0.95 * spun[s, part, cols].astype(F32) + grad).astype(BF)
                spun[s, part, cols] = moment
                value = grad + 0.95 * moment.astype(F32)
                nest[part, cols] = value
                total = total + jnp.sum(value * value, axis=0, keepdims=True)
            return total

        total = lax.fori_loop(0, width // 128, start, jnp.zeros((1, 128), F32))
        scale = 1.0 / (jnp.sqrt(jnp.sum(total, axis=1, keepdims=True)) + 1e-07)

        @pl.loop(0, width // 256)
        def _(n):
            cols = tile_cols(n, 256)
            x[:, cols] = (nest[:, cols] * scale).astype(BF)

        def mix():
            @pl.loop(0, pad // 256)
            def _(n):
                cols = tile_cols(n, 256)
                gram[:, cols] = mm(x[...], x[cols, :], ((1,), (1,))).astype(BF)

            @pl.loop(0, pad // 256)
            def _(n):
                cols = tile_cols(n, 256)
                part = gram[:, cols]
                square = mm(gram[...], part)
                mixed[:, cols] = (-4.775 * part.astype(F32) + 2.0315 * square).astype(BF)

        def product():
            @pl.loop(0, width // 256)
            def _(n):
                cols = tile_cols(n, 256)
                part = x[:, cols]
                x[:, cols] = (3.4445 * part.astype(F32) + mm(mixed[...], part)).astype(BF)

        for _ in range(ITERS - 1):
            mix()
            product()
        mix()
        before_last()
        product()
        factor = 0.2 * max(hid, width) ** 0.5

        @pl.loop(0, nr // 2)
        def _(q):
            cols = tile_cols(q, 128)
            both = jnp.concatenate(
                [(factor * x[h * upper : (h + 1) * upper, cols].astype(F32)).astype(BF) for h in range(2)], axis=1
            )
            out = mm(both, swap[...])
            for i in range(2):
                w_buf[s, pl.ds((2 * q + i) * nf, nf)] = (
                    out[:, 128 * i : 128 * i + 128].reshape(nf, blk, 128).astype(BF)
                )

    def ungroup(s):
        def one(dz):
            k = lax.rem(z + dz, nz)
            wait_bytes(u_buf.at[s, pl.ds(2 * k * nr, 2 * nr)], out_recv.at[s, k])
            pair = jnp.concatenate(
                [u_buf[s, pl.ds((2 * k + i) * nr, nr)].reshape(nr * blk, 128) for i in range(2)], axis=1
            )
            out = mm(regroup_t[...], pair).astype(BF)
            s_buf[s, 2 * k] = out[:, :128].reshape(half, nr, 128)
            s_buf[s, 2 * k + 1] = out[:, 128:].reshape(half, nr, 128)

        @pl.loop(0, nz // 2 - 1)
        def _(k):
            one(k + 1)
            one(nz - 1 - k)

        @pl.loop(0, 2)
        def _(k):
            one(k * (nz // 2))

    def along_z(src, dst, send_sem, recv_sem):
        pltpu.make_async_copy(src.at[z], dst.at[z], recv_sem).start()

        def send(dz):
            to_z = lax.rem(z + dz, nz)
            pltpu.make_async_remote_copy(
                src.at[to_z], dst.at[z], send_sem, recv_sem,
                device_id=(rep, 2 * to_z + core), device_id_type=MESH,
            ).start()

        send(nz // 2)
        for k in range(nz // 2 - 1, 0, -1):
            send(k)
            send(nz - k)

    def in_plane(visit):
        visit(2 * rep + 1 - core, rep, 2 * z + 1 - core)

        @pl.loop(1, nr)
        def _(j):
            to_r = moved(j)
            for dc in range(2):
                to_c = lax.rem(core + dc, 2)
                visit(2 * to_r + to_c, to_r, 2 * z + to_c)

    def relay_in():
        @pl.loop(0, nz // 2)
        def _(k):
            pair = jnp.concatenate([zr_buf[2 * k + i].reshape(half * nr, 128) for i in range(2)], axis=1)
            out = mm(spread_in[...], pair)
            for i in range(2):
                zt_buf[:, 2 * k + i] = out[:, 128 * i : 128 * i + 128].reshape(2 * nr, blk, 128).astype(BF)

        def send(to, to_r, to_f):
            pltpu.make_async_remote_copy(
                zt_buf.at[to], v_buf.at[1, pl.ds(rep * nf + core * nz, nz)], p_send, in_recv.at[1],
                device_id=(to_r, to_f), device_id_type=MESH,
            ).start()

        pltpu.make_async_copy(
            zt_buf.at[2 * rep + core], v_buf.at[1, pl.ds(rep * nf + core * nz, nz)], in_recv.at[1]
        ).start()
        in_plane(send)

    def plane_out():
        def send(to, to_r, to_f):
            pltpu.make_async_remote_copy(
                w_buf.at[1, pl.ds(to * nz, nz)], zv_buf.at[2 * rep + core], po_send, po_recv,
                device_id=(to_r, to_f), device_id_type=MESH,
            ).start()

        pltpu.make_async_copy(w_buf.at[1, pl.ds((2 * rep + core) * nz, nz)], zv_buf.at[2 * rep + core], po_recv).start()
        in_plane(send)

    def relay_out():
        @pl.loop(0, nz // 2)
        def _(k):
            pair = jnp.concatenate(
                [zv_buf[:, 2 * k + i].reshape(2 * nr * blk, 128) for i in range(2)], axis=1
            )
            out = mm(spread_out[...], pair).astype(BF)
            for i in range(2):
                zs_buf[2 * k + i] = out[:, 128 * i : 128 * i + 128].reshape(half, nr, 128)

    def block(a):
        return pl.ds(pl.multiple_of(lax.rem(a, 6) * 128, 128), 128), tile_cols(a // 6, 256)

    def unpack_second(tile):
        chosen = select(1)

        @pl.loop(0, half)
        def _(a):
            nest[block(a)] = mm(tile(a), chosen, ((0,), (0,)))

    def unpack():
        chosen = select(0)

        @pl.loop(0, half)
        def _(a):
            first = mm(s_buf[0, :, a].reshape(mats, 128), chosen, ((0,), (0,)))
            out = (first + nest[block(a)]).astype(BF)
            upd_ref[a] = out[0:64]
            upd_ref[a + half] = out[64:128]

    def all_but_one(ref):
        return ref.at[pl.ds(0, ref.shape[0] - 1)]

    loads[0].wait()
    if relayed:
        gather(1, True)
        pl.semaphore_wait(barrier, mats - 1)
        along_z(zs_buf, zr_buf, z_send, z_recv)
        gather(0, False)
        relay_matrices()
        for load in loads[1:]:
            load.wait()
        regroup_all(0)
        spin_momentum(1)
        spin_momentum(0)

        wait_bytes(zr_buf, z_recv)
        relay_in()
        send_in(0, True)
        wait_bytes(v_buf.at[1], in_recv.at[1])
        orthogonalize(1, lambda: None)
        plane_out()

        wait_bytes(v_buf.at[0], in_recv.at[0])
        def second_back():
            wait_bytes(zv_buf, po_recv)
            wait_bytes(all_but_one(zs_buf), z_send)
            relay_out()
            along_z(zs_buf, zu_buf, zo_send, zo_recv)

        orthogonalize(0, second_back)
        send_out(0)
        store_momentum(1)
        store_momentum(0)
        wait_bytes(zu_buf, zo_recv)
        unpack_second(lambda a: zu_buf[:, a].reshape(nz * nr, 128))
        ungroup(0)
        unpack()
        wait_bytes(all_but_one(zt_buf), p_send)
        wait_bytes(all_but_one(zv_buf), po_send)
        wait_bytes(all_but_one(zs_buf), zo_send)
    else:
        gather(0, True)
        for load in loads[1:]:
            load.wait()
        pl.semaphore_wait(barrier, mats - 1)
        send_in(0, False)
        gather(1, False)
        send_in(1, False)
        spin_momentum(0)
        spin_momentum(1)
        for s in range(2):
            wait_bytes(v_buf.at[s], in_recv.at[s])
            orthogonalize(s, lambda: None)
            send_out(s)
        for s in range(2):
            store_momentum(s)
        ungroup(1)
        unpack_second(lambda a: s_buf[1, :, a].reshape(mats, 128))
        ungroup(0)
        unpack()

    for s in range(2):
        wait_bytes(new.at[s], new_sem.at[s])
    for s in range(1 if relayed else 2):
        wait_bytes(all_but_one(t_buf.at[s]), in_send.at[s])
        wait_bytes(all_but_one(w_buf.at[s]), out_send.at[s])


def one_hot(rows, cols, pairs):
    out = np.zeros((rows, cols), np.float32)
    for i, j in pairs:
        out[i, j] = 1.0
    return jnp.asarray(out, BF)


def on_device(grads, momentum, owner):
    nf, nr = lax.axis_size("fsdp"), lax.axis_size("rep")
    mats, tile_rows, tile_cols = grads.shape
    half = tile_rows // 2
    hid, width = nf * tile_rows, nr * tile_cols
    blk = half + 2
    upper = nf * blk
    pad = 2 * upper
    nz = nf // 2

    regroup_pairs = [(r * blk + a, a * nr + r) for r in range(nr) for a in range(half)]
    row_pairs = [
        (tile_rows * f + half * h + a, h * upper + (f % 2 * nz + f // 2) * blk + a)
        for f in range(nf) for h in range(2) for a in range(half)
    ]
    swap_pairs = [(i * 128 + j * 64 + c, j * 128 + i * 64 + c) for i in range(2) for j in range(2) for c in range(64)]
    flip = lambda pairs: [(j, i) for i, j in pairs]
    regroup = one_hot(nr * blk, half * nr, regroup_pairs)
    regroup_t = one_hot(half * nr, nr * blk, flip(regroup_pairs))
    rows = one_hot(pad, pad, row_pairs)
    rows_t = one_hot(pad, pad, flip(row_pairs))
    swap = one_hot(256, 256, swap_pairs)

    vmem = pl.BlockSpec(memory_space=pltpu.VMEM)
    hbm = pl.BlockSpec(memory_space=pl.ANY)
    cfg = (nr, nf, half, hid, width, pad)
    turned = grads.transpose(1, 2, 0)
    tables = [regroup, regroup_t, rows, rows_t, swap]
    by_f = pltpu.VMEM((2, nf, half, nr, 128), BF)
    tiles = pltpu.VMEM((2, mats, blk, 128), BF)
    by_z = pltpu.VMEM((nz, half, nr, 128), BF)
    in_plane = pltpu.VMEM((2 * nr, nz, blk, 128), BF)
    one = pltpu.SemaphoreType.DMA(())
    relay_scratch = [
        by_z, by_z, in_plane, in_plane, by_z,
        pltpu.VMEM((2 * nr * blk, half * nr), BF),
        pltpu.VMEM((half * nr, 2 * nr * blk), BF),
        *[one for _ in range(7)],
    ]

    def run(relayed, operands):
        return pl.pallas_call(
            functools.partial(kernel, cfg, relayed),
            out_shape=(
                jax.ShapeDtypeStruct((tile_rows, tile_cols, mats), BF),
                jax.ShapeDtypeStruct(momentum.shape[1:], BF),
            ),
            in_specs=[vmem] + [hbm] * 7,
            out_specs=(vmem, hbm),
            scratch_shapes=[
                pltpu.VMEM(turned.shape, BF),
                *[pltpu.VMEM(table.shape, BF) for table in tables],
                pltpu.VMEM((2, mats), jnp.int32),
                by_f, tiles, tiles, tiles, tiles,
                pltpu.VMEM((2, pad, width), BF),
                pltpu.VMEM((2, pad, width), BF),
                pltpu.VMEM((2, hid, width), BF),
                pltpu.VMEM((pad, width), F32),
                pltpu.VMEM((pad, width), BF),
                pltpu.VMEM((pad, pad), BF),
                pltpu.VMEM((pad, pad), BF),
                pltpu.SemaphoreType.DMA((6,)),
                *[pltpu.SemaphoreType.DMA((2,)) for _ in range(5)],
                pltpu.SemaphoreType.DMA((2, nz)),
                *(relay_scratch if relayed else []),
            ],
            compiler_params=pltpu.CompilerParams(
                collective_id=1 if relayed else 0, has_side_effects=True, vmem_limit_bytes=58 * 1024 * 1024
            ),
            name="muon_relayed" if relayed else "muon_direct",
        )(*operands)

    order = jnp.arange(mats, dtype=jnp.int32)
    second = (owner[:, None] == owner[None, :]) & (order[:, None] < order[None, :])
    plane = (owner % nf) // 2
    in_each = second[None] & (plane[None, None, :] == jnp.arange(nz, dtype=jnp.int32)[:, None, None])
    fits = jnp.max(jnp.sum(in_each.astype(jnp.int32), axis=(1, 2))) <= nr
    operands = (owner[None, :], turned, momentum[0], *tables)
    update, new = lax.cond(fits, functools.partial(run, True), functools.partial(run, False), operands)
    return (update.transpose(2, 0, 1), new[None])


def solution(mesh):
    return jax.shard_map(
        on_device,
        mesh=mesh,
        in_specs=(P(None, "fsdp", "rep"), P(("rep", "fsdp"), None, None, None), P()),
        out_specs=(P(None, "fsdp", "rep"), P(("rep", "fsdp"), None, None, None)),
        check_vma=False,
    )
```

```python
import functools

import jax
import jax.numpy as jnp
import numpy as np
from jax import lax
from jax.experimental import pallas as pl
from jax.experimental.pallas import tpu as pltpu
from jax.sharding import PartitionSpec as P

ITERS = 2
MESH = pl.DeviceIdType.MESH
BF = jnp.bfloat16
F32 = jnp.float32


def mm(a, b, dims=((1,), (0,))):
    return lax.dot_general(a, b, (dims, ((), ())), preferred_element_type=F32)


def wait_bytes(ref, sem):
    pltpu.make_async_copy(ref, ref, sem).wait()


def tile_cols(n, size):
    return pl.ds(pl.multiple_of(n * size, size), size)


def kernel(
    cfg, relayed,
    owner_ref, g_hbm, mom_hbm, regroup_hbm, regroup_t_hbm, rows_hbm, rows_t_hbm, swap_hbm,
    upd_ref, new_hbm,
    g, regroup, regroup_t, rows, rows_t, swap, keys,
    s_buf, t_buf, v_buf, w_buf, u_buf, mom, spun, new, nest, x, gram, mixed,
    load_sem, mom_sem, new_sem, in_send, in_recv, out_send, out_recv,
    *relay_refs,
):
    nr, nf, half, hid, width, pad = cfg
    rep, fs = lax.axis_index("rep"), lax.axis_index("fsdp")
    mats = nr * nf
    blk = half + 2
    upper = nf * blk
    nz = nf // 2
    z, core = fs // 2, lax.rem(fs, 2)
    lane = rep * nf + core * nz + z
    if relayed:
        (zs_buf, zr_buf, zt_buf, zv_buf, zu_buf, spread_in, spread_out,
         z_send, z_recv, p_send, zo_send, zo_recv, po_send, po_recv) = relay_refs

    loads = [(g_hbm, g), (regroup_hbm, regroup), (swap_hbm, swap), (rows_hbm, rows),
             (rows_t_hbm, rows_t), (regroup_t_hbm, regroup_t)]
    loads = [pltpu.make_async_copy(a, b, load_sem.at[i]) for i, (a, b) in enumerate(loads)]
    for load in loads:
        load.start()
    for s in range(2):
        pltpu.make_async_copy(mom_hbm.at[s], mom.at[s, pl.ds(0, hid)], mom_sem.at[s]).start()

    side = 4
    rx, ry = rep // side, lax.rem(rep, side)

    def moved(j):
        return lax.rem(rx + j, side) * side + lax.rem(ry + j // side + j, side)

    def faces(dz, dc):
        return 2 * lax.rem(z + dz, nz) + lax.rem(core + dc, 2)

    def everyone(visit):
        @pl.loop(0, nz // 2 - 1)
        def _(k):
            @pl.loop(0, nr)
            def _(j):
                to_r = moved(j)
                for dc in range(2):
                    visit(to_r, faces(k + 1, dc))
                    visit(to_r, faces(nz - 1 - k, dc))

        for dc in range(2):
            visit(rep, faces(nz // 2, dc))
        visit(rep, faces(0, 1))

        @pl.loop(1, nr)
        def _(j):
            to_r = moved(j)
            for dc in range(2):
                visit(to_r, faces(nz // 2, dc))
                visit(to_r, faces(0, dc))

    barrier = pltpu.get_barrier_semaphore()

    def greet(to_r, to_f):
        pl.semaphore_signal(barrier, inc=1, device_id=(to_r, to_f), device_id_type=MESH)

    everyone(greet)

    owner = owner_ref[...]
    down = jnp.transpose(jnp.broadcast_to(owner, (mats, mats)))
    index = lax.broadcasted_iota(jnp.int32, (mats, mats), 0)
    order = lax.broadcasted_iota(jnp.int32, (mats, mats), 1)
    earlier = (down == owner) & (index < order)
    slot = jnp.sum(jnp.where(earlier, 1, 0), axis=0, keepdims=True)
    place = (owner % nf) * nr + owner // nf
    keys[0:1, :] = jnp.where(slot == 0, place, -1)
    if relayed:
        plane = jnp.where(slot == 1, (owner % nf) // 2, -1)
        plane_down = jnp.transpose(jnp.broadcast_to(plane, (mats, mats)))
        before = (plane_down == plane) & (index < order)
        rank = jnp.sum(jnp.where(before, 1, 0), axis=0, keepdims=True)
        keys[1:2, :] = jnp.where(slot == 1, plane * nr + rank, -1)
    else:
        keys[1:2, :] = jnp.where(slot == 1, place, -1)

    def relay_matrices():
        member = (owner // nf) * 2 + owner % 2 + 1
        wide = half * nr
        column = lax.broadcasted_iota(jnp.int32, (wide, mats), 0) % nr
        here = jnp.where(keys[1:2, :] == z * nr + column, 1.0, 0.0).astype(BF)
        members = jnp.broadcast_to(member, (8, mats)).astype(F32).astype(BF)
        owner_of = mm(members, here, ((1,), (1,)))[0:1, :]
        line = lax.broadcasted_iota(jnp.int32, (2 * nr * blk, wide), 0)
        source = lax.broadcasted_iota(jnp.int32, (2 * nr * blk, wide), 1)
        wanted = (owner_of == (line // blk + 1).astype(F32)) & (line % blk == source // nr)
        wanted = jnp.where(wanted, 1.0, 0.0)
        spread_in[...] = wanted.astype(BF)
        spread_out[...] = jnp.transpose(wanted).astype(BF)

    few = 2 if relayed else 1

    def select(s):
        places = nz * nr if relayed and s == 1 else mats
        slot_id = lax.broadcasted_iota(jnp.int32, (places, mats), 0)
        return jnp.where(slot_id == keys[s : s + 1, :], 1.0, 0.0).astype(BF)

    def gather(s):
        chosen = select(s)

        @pl.loop(0, half // 2, unroll=half // 2 if relayed else 1)
        def _(k):
            both = jnp.concatenate([g[2 * k], g[2 * k + half], g[2 * k + 1], g[2 * k + 1 + half]], axis=0)
            out = mm(chosen, both, ((1,), (1,))).astype(BF)
            for i in range(2):
                part = out[:, 128 * i : 128 * i + 128]
                if relayed and s == 1:
                    zs_buf[:, 2 * k + i] = part.reshape(nz, nr, 128)
                else:
                    s_buf[s, :, 2 * k + i] = part.reshape(nf, nr, 128)

    def regroup_two(s, k):
        first, second = k, k + 1
        pair = jnp.concatenate(
            [s_buf[s, first].reshape(half * nr, 128), s_buf[s, second].reshape(half * nr, 128)], axis=1
        )
        out = mm(regroup[...], pair)
        t_buf[s, pl.ds(first * nr, nr)] = out[:, :128].reshape(nr, blk, 128).astype(BF)
        t_buf[s, pl.ds(second * nr, nr)] = out[:, 128:].reshape(nr, blk, 128).astype(BF)

    def regroup_all(s):
        @pl.loop(0, nf // 2, unroll=few)
        def _(k):
            regroup_two(s, 2 * k)

    def send_in(s, regrouped):
        def send(to_r, to_f):
            pltpu.make_async_remote_copy(
                t_buf.at[s, to_f * nr + to_r], v_buf.at[s, lane], in_send.at[s], in_recv.at[s],
                device_id=(to_r, to_f), device_id_type=MESH,
            ).start()

        if not regrouped:
            regroup_all(s)
        pltpu.make_async_copy(t_buf.at[s, fs * nr + rep], v_buf.at[s, lane], in_recv.at[s]).start()
        everyone(send)

    def send_out(s):
        def send(to_r, to_f):
            pltpu.make_async_remote_copy(
                w_buf.at[s, to_r * nf + lax.rem(to_f, 2) * nz + to_f // 2], u_buf.at[s, fs * nr + rep], out_send.at[s], out_recv.at[s],
                device_id=(to_r, to_f), device_id_type=MESH,
            ).start()

        pltpu.make_async_copy(w_buf.at[s, lane], u_buf.at[s, fs * nr + rep], out_recv.at[s]).start()
        everyone(send)

    def spin_momentum(s):
        wait_bytes(mom.at[s, pl.ds(0, hid)], mom_sem.at[s])
        if pad > hid:
            mom[s, hid:pad, :] = jnp.zeros((pad - hid, width), BF)

        @pl.loop(0, width // 256)
        def _(n):
            cols = tile_cols(n, 256)
            spun[s, :, cols] = mm(rows_t[...], mom[s, :, cols]).astype(BF)

    def store_momentum(s):
        own = rep * nf + fs
        mine = jnp.sum(jnp.where(owner_ref[...] == own, 1, 0), axis=1, keepdims=True)
        owned = mine > s

        @pl.loop(0, width // 256)
        def _(n):
            cols = tile_cols(n, 256)
            moment = mm(rows[0:hid, :], spun[s, :, cols])
            new[s, :, cols] = jnp.where(owned, moment, mom[s, 0:hid, cols].astype(F32)).astype(BF)

        pltpu.make_async_copy(new.at[s], new_hbm.at[s], new_sem.at[s]).start()

    def orthogonalize(s):
        def start(q, total):
            pair = jnp.concatenate(
                [v_buf[s, pl.ds((2 * q + i) * nf, nf)].reshape(upper, 128) for i in range(2)], axis=1
            )
            both = mm(pair, swap[...])
            cols = tile_cols(q, 128)
            for h in range(2):
                part = slice(h * upper, (h + 1) * upper)
                grad = both[:, 128 * h : 128 * h + 128]
                moment = (0.95 * spun[s, part, cols].astype(F32) + grad).astype(BF)
                spun[s, part, cols] = moment
                value = grad + 0.95 * moment.astype(F32)
                nest[part, cols] = value
                total = total + jnp.sum(value * value, axis=0, keepdims=True)
            return total

        total = lax.fori_loop(0, width // 128, start, jnp.zeros((1, 128), F32), unroll=2 * few)
        scale = 1.0 / (jnp.sqrt(jnp.sum(total, axis=1, keepdims=True)) + 1e-07)

        @pl.loop(0, width // 256, unroll=few)
        def _(n):
            cols = tile_cols(n, 256)
            x[:, cols] = (nest[:, cols] * scale).astype(BF)

        @pl.loop(0, ITERS)
        def _(turn):
            def columns(count, step):
                if relayed:
                    for n in range(count):
                        step(slice(256 * n, 256 * n + 256))
                else:
                    pl.loop(0, count)(lambda n: step(tile_cols(n, 256)))

            def to_gram(cols):
                gram[:, cols] = mm(x[...], x[cols, :], ((1,), (1,))).astype(BF)

            def to_mixed(cols):
                part = gram[:, cols]
                square = mm(gram[...], part)
                mixed[:, cols] = (-4.775 * part.astype(F32) + 2.0315 * square).astype(BF)

            def to_x(cols):
                part = x[:, cols]
                product = mm(mixed[...], part)
                x[:, cols] = (3.4445 * part.astype(F32) + product).astype(BF)

            columns(pad // 256, to_gram)
            columns(pad // 256, to_mixed)
            columns(width // 256, to_x)

        factor = 0.2 * max(hid, width) ** 0.5

        @pl.loop(0, nr // 2, unroll=2 * few)
        def _(q):
            cols = tile_cols(q, 128)
            both = jnp.concatenate(
                [(factor * x[h * upper : (h + 1) * upper, cols].astype(F32)).astype(BF) for h in range(2)], axis=1
            )
            out = mm(both, swap[...])
            for i in range(2):
                w_buf[s, pl.ds((2 * q + i) * nf, nf)] = (
                    out[:, 128 * i : 128 * i + 128].reshape(nf, blk, 128).astype(BF)
                )

    def ungroup(s):
        @pl.loop(0, nf // 2, unroll=few)
        def _(k):
            pair = jnp.concatenate(
                [u_buf[s, pl.ds((2 * k + i) * nr, nr)].reshape(nr * blk, 128) for i in range(2)], axis=1
            )
            out = mm(regroup_t[...], pair).astype(BF)
            s_buf[s, 2 * k] = out[:, :128].reshape(half, nr, 128)
            s_buf[s, 2 * k + 1] = out[:, 128:].reshape(half, nr, 128)

    def along_z(src, dst, send_sem, recv_sem):
        pltpu.make_async_copy(src.at[z], dst.at[z], recv_sem).start()

        def send(dz):
            to_z = lax.rem(z + dz, nz)
            pltpu.make_async_remote_copy(
                src.at[to_z], dst.at[z], send_sem, recv_sem,
                device_id=(rep, 2 * to_z + core), device_id_type=MESH,
            ).start()

        send(nz // 2)
        for k in range(nz // 2 - 1, 0, -1):
            send(k)
            send(nz - k)

    def in_plane(visit):
        visit(2 * rep + 1 - core, rep, 2 * z + 1 - core)

        @pl.loop(1, nr)
        def _(j):
            to_r = moved(j)
            for dc in range(2):
                to_c = lax.rem(core + dc, 2)
                visit(2 * to_r + to_c, to_r, 2 * z + to_c)

    def relay_in():
        @pl.loop(0, nz // 2, unroll=few)
        def _(k):
            pair = jnp.concatenate([zr_buf[2 * k + i].reshape(half * nr, 128) for i in range(2)], axis=1)
            out = mm(spread_in[...], pair)
            for i in range(2):
                zt_buf[:, 2 * k + i] = out[:, 128 * i : 128 * i + 128].reshape(2 * nr, blk, 128).astype(BF)

        def send(to, to_r, to_f):
            pltpu.make_async_remote_copy(
                zt_buf.at[to], v_buf.at[1, pl.ds(rep * nf + core * nz, nz)], p_send, in_recv.at[1],
                device_id=(to_r, to_f), device_id_type=MESH,
            ).start()

        pltpu.make_async_copy(
            zt_buf.at[2 * rep + core], v_buf.at[1, pl.ds(rep * nf + core * nz, nz)], in_recv.at[1]
        ).start()
        in_plane(send)

    def plane_out():
        def send(to, to_r, to_f):
            pltpu.make_async_remote_copy(
                w_buf.at[1, pl.ds(to * nz, nz)], zv_buf.at[2 * rep + core], po_send, po_recv,
                device_id=(to_r, to_f), device_id_type=MESH,
            ).start()

        pltpu.make_async_copy(w_buf.at[1, pl.ds((2 * rep + core) * nz, nz)], zv_buf.at[2 * rep + core], po_recv).start()
        in_plane(send)

    def relay_out():
        @pl.loop(0, nz // 2, unroll=few)
        def _(k):
            pair = jnp.concatenate(
                [zv_buf[:, 2 * k + i].reshape(2 * nr * blk, 128) for i in range(2)], axis=1
            )
            out = mm(spread_out[...], pair).astype(BF)
            for i in range(2):
                zs_buf[2 * k + i] = out[:, 128 * i : 128 * i + 128].reshape(half, nr, 128)

    def unpack(second):
        chosen = jnp.concatenate([select(0), select(1)], axis=0)

        @pl.loop(0, half // 2, unroll=half // 2 if relayed else 1)
        def _(k):
            tiles = [
                jnp.concatenate([s_buf[0, :, 2 * k + i].reshape(mats, 128), second(2 * k + i)], axis=0) for i in range(2)
            ]
            out = mm(jnp.concatenate(tiles, axis=1), chosen, ((0,), (0,))).astype(BF)
            for i in range(2):
                upd_ref[2 * k + i] = out[128 * i : 128 * i + 64]
                upd_ref[2 * k + i + half] = out[128 * i + 64 : 128 * i + 128]

    def all_but_one(ref):
        return ref.at[pl.ds(0, ref.shape[0] - 1)]

    loads[0].wait()
    if relayed:
        gather(1)
        pl.semaphore_wait(barrier, mats - 1)
        along_z(zs_buf, zr_buf, z_send, z_recv)
        gather(0)
        for load in loads[1:]:
            load.wait()
        regroup_all(0)
        relay_matrices()
        spin_momentum(1)
        spin_momentum(0)

        wait_bytes(zr_buf, z_recv)
        relay_in()
        send_in(0, True)
        wait_bytes(v_buf.at[1], in_recv.at[1])
        orthogonalize(1)
        plane_out()

        wait_bytes(v_buf.at[0], in_recv.at[0])
        orthogonalize(0)
        send_out(0)

        wait_bytes(zv_buf, po_recv)
        wait_bytes(all_but_one(zs_buf), z_send)
        relay_out()
        along_z(zs_buf, zu_buf, zo_send, zo_recv)
        store_momentum(1)
        store_momentum(0)

        wait_bytes(u_buf.at[0], out_recv.at[0])
        ungroup(0)
        wait_bytes(zu_buf, zo_recv)
        unpack(lambda a: zu_buf[:, a].reshape(nz * nr, 128))
        wait_bytes(all_but_one(zt_buf), p_send)
        wait_bytes(all_but_one(zv_buf), po_send)
        wait_bytes(all_but_one(zs_buf), zo_send)
    else:
        gather(0)
        for load in loads[1:]:
            load.wait()
        pl.semaphore_wait(barrier, mats - 1)
        send_in(0, False)
        gather(1)
        send_in(1, False)
        spin_momentum(0)
        spin_momentum(1)
        for s in range(2):
            wait_bytes(v_buf.at[s], in_recv.at[s])
            orthogonalize(s)
            send_out(s)
        for s in range(2):
            store_momentum(s)
        for s in range(2):
            wait_bytes(u_buf.at[s], out_recv.at[s])
            ungroup(s)
        unpack(lambda a: s_buf[1, :, a].reshape(mats, 128))

    for s in range(2):
        wait_bytes(new.at[s], new_sem.at[s])
    for s in range(1 if relayed else 2):
        wait_bytes(all_but_one(t_buf.at[s]), in_send.at[s])
        wait_bytes(all_but_one(w_buf.at[s]), out_send.at[s])


def one_hot(rows, cols, pairs):
    out = np.zeros((rows, cols), np.float32)
    for i, j in pairs:
        out[i, j] = 1.0
    return jnp.asarray(out, BF)


def on_device(grads, momentum, owner):
    nf, nr = lax.axis_size("fsdp"), lax.axis_size("rep")
    mats, tile_rows, tile_cols = grads.shape
    half = tile_rows // 2
    hid, width = nf * tile_rows, nr * tile_cols
    blk = half + 2
    upper = nf * blk
    pad = 2 * upper
    nz = nf // 2

    regroup_pairs = [(r * blk + a, a * nr + r) for r in range(nr) for a in range(half)]
    row_pairs = [
        (tile_rows * f + half * h + a, h * upper + (f % 2 * nz + f // 2) * blk + a)
        for f in range(nf) for h in range(2) for a in range(half)
    ]
    swap_pairs = [(i * 128 + j * 64 + c, j * 128 + i * 64 + c) for i in range(2) for j in range(2) for c in range(64)]
    flip = lambda pairs: [(j, i) for i, j in pairs]
    regroup = one_hot(nr * blk, half * nr, regroup_pairs)
    regroup_t = one_hot(half * nr, nr * blk, flip(regroup_pairs))
    rows = one_hot(pad, pad, row_pairs)
    rows_t = one_hot(pad, pad, flip(row_pairs))
    swap = one_hot(256, 256, swap_pairs)

    vmem = pl.BlockSpec(memory_space=pltpu.VMEM)
    hbm = pl.BlockSpec(memory_space=pl.ANY)
    cfg = (nr, nf, half, hid, width, pad)
    turned = grads.transpose(1, 2, 0)
    tables = [regroup, regroup_t, rows, rows_t, swap]
    by_f = pltpu.VMEM((2, nf, half, nr, 128), BF)
    tiles = pltpu.VMEM((2, mats, blk, 128), BF)
    by_z = pltpu.VMEM((nz, half, nr, 128), BF)
    in_plane = pltpu.VMEM((2 * nr, nz, blk, 128), BF)
    one = pltpu.SemaphoreType.DMA(())
    relay_scratch = [
        by_z, by_z, in_plane, in_plane, by_z,
        pltpu.VMEM((2 * nr * blk, half * nr), BF),
        pltpu.VMEM((half * nr, 2 * nr * blk), BF),
        *[one for _ in range(7)],
    ]

    def run(relayed, operands):
        return pl.pallas_call(
            functools.partial(kernel, cfg, relayed),
            out_shape=(
                jax.ShapeDtypeStruct((tile_rows, tile_cols, mats), BF),
                jax.ShapeDtypeStruct(momentum.shape[1:], BF),
            ),
            in_specs=[vmem] + [hbm] * 7,
            out_specs=(vmem, hbm),
            scratch_shapes=[
                pltpu.VMEM(turned.shape, BF),
                *[pltpu.VMEM(table.shape, BF) for table in tables],
                pltpu.VMEM((2, mats), jnp.int32),
                by_f, tiles, tiles, tiles, tiles,
                pltpu.VMEM((2, pad, width), BF),
                pltpu.VMEM((2, pad, width), BF),
                pltpu.VMEM((2, hid, width), BF),
                pltpu.VMEM((pad, width), F32),
                pltpu.VMEM((pad, width), BF),
                pltpu.VMEM((pad, pad), BF),
                pltpu.VMEM((pad, pad), BF),
                pltpu.SemaphoreType.DMA((6,)),
                *[pltpu.SemaphoreType.DMA((2,)) for _ in range(6)],
                *(relay_scratch if relayed else []),
            ],
            compiler_params=pltpu.CompilerParams(
                collective_id=1 if relayed else 0, has_side_effects=True, vmem_limit_bytes=58 * 1024 * 1024
            ),
            name="muon_relayed" if relayed else "muon_direct",
        )(*operands)

    order = jnp.arange(mats, dtype=jnp.int32)
    second = (owner[:, None] == owner[None, :]) & (order[:, None] < order[None, :])
    plane = (owner % nf) // 2
    in_each = second[None] & (plane[None, None, :] == jnp.arange(nz, dtype=jnp.int32)[:, None, None])
    fits = jnp.max(jnp.sum(in_each.astype(jnp.int32), axis=(1, 2))) <= nr
    operands = (owner[None, :], turned, momentum[0], *tables)
    update, new = lax.cond(fits, functools.partial(run, True), functools.partial(run, False), operands)
    return (update.transpose(2, 0, 1), new[None])


def solution(mesh):
    return jax.shard_map(
        on_device,
        mesh=mesh,
        in_specs=(P(None, "fsdp", "rep"), P(("rep", "fsdp"), None, None, None), P()),
        out_specs=(P(None, "fsdp", "rep"), P(("rep", "fsdp"), None, None, None)),
        check_vma=False,
    )
```

```python
import functools

import jax
import jax.numpy as jnp
import numpy as np
from jax import lax
from jax.experimental import pallas as pl
from jax.experimental.pallas import tpu as pltpu
from jax.sharding import PartitionSpec as P

ITERS = 2
MESH = pl.DeviceIdType.MESH
BF = jnp.bfloat16
F32 = jnp.float32


def mm(a, b, dims=((1,), (0,))):
    return lax.dot_general(a, b, (dims, ((), ())), preferred_element_type=F32)


def wait_bytes(ref, sem):
    pltpu.make_async_copy(ref, ref, sem).wait()


def tile_cols(n, size):
    return pl.ds(pl.multiple_of(n * size, size), size)


def kernel(
    cfg, relayed,
    owner_ref, g_hbm, mom_hbm, regroup_hbm, regroup_t_hbm, rows_hbm, rows_t_hbm, swap_hbm,
    upd_ref, new_hbm,
    g, regroup, regroup_t, rows, rows_t, swap, keys,
    s_buf, t_buf, v_buf, w_buf, u_buf, mom, spun, new, nest, x, gram, mixed,
    load_sem, mom_sem, new_sem, in_send, in_recv, out_send, out_recv,
    *relay_refs,
):
    nr, nf, half, hid, width, pad = cfg
    rep, fs = lax.axis_index("rep"), lax.axis_index("fsdp")
    mats = nr * nf
    blk = half + 2
    upper = nf * blk
    nz = nf // 2
    z, core = fs // 2, lax.rem(fs, 2)
    lane = rep * nf + core * nz + z
    if relayed:
        (zs_buf, zr_buf, zt_buf, zv_buf, zu_buf, spread_in, spread_out,
         z_send, z_recv, p_send, zo_send, zo_recv, po_send, po_recv) = relay_refs

    loads = [(g_hbm, g), (regroup_hbm, regroup), (swap_hbm, swap), (rows_hbm, rows),
             (rows_t_hbm, rows_t), (regroup_t_hbm, regroup_t)]
    loads = [pltpu.make_async_copy(a, b, load_sem.at[i]) for i, (a, b) in enumerate(loads)]
    for load in loads:
        load.start()
    for s in range(2):
        pltpu.make_async_copy(mom_hbm.at[s], mom.at[s, pl.ds(0, hid)], mom_sem.at[s]).start()

    side = 4
    rx, ry = rep // side, lax.rem(rep, side)

    def moved(j):
        return lax.rem(rx + j, side) * side + lax.rem(ry + j // side + j, side)

    def faces(dz, dc):
        return 2 * lax.rem(z + dz, nz) + lax.rem(core + dc, 2)

    def everyone(visit):
        @pl.loop(0, nz // 2 - 1)
        def _(k):
            @pl.loop(0, nr)
            def _(j):
                to_r = moved(j)
                for dc in range(2):
                    visit(to_r, faces(k + 1, dc))
                    visit(to_r, faces(nz - 1 - k, dc))

        for dc in range(2):
            visit(rep, faces(nz // 2, dc))
        visit(rep, faces(0, 1))

        @pl.loop(1, nr)
        def _(j):
            to_r = moved(j)
            for dc in range(2):
                visit(to_r, faces(nz // 2, dc))
                visit(to_r, faces(0, dc))

    barrier = pltpu.get_barrier_semaphore()

    def greet(to_r, to_f):
        pl.semaphore_signal(barrier, inc=1, device_id=(to_r, to_f), device_id_type=MESH)

    everyone(greet)

    owner = owner_ref[...]
    down = jnp.transpose(jnp.broadcast_to(owner, (mats, mats)))
    index = lax.broadcasted_iota(jnp.int32, (mats, mats), 0)
    order = lax.broadcasted_iota(jnp.int32, (mats, mats), 1)
    earlier = (down == owner) & (index < order)
    slot = jnp.sum(jnp.where(earlier, 1, 0), axis=0, keepdims=True)
    place = (owner % nf) * nr + owner // nf
    keys[0:1, :] = jnp.where(slot == 0, place, -1)
    if relayed:
        plane = jnp.where(slot == 1, (owner % nf) // 2, -1)
        plane_down = jnp.transpose(jnp.broadcast_to(plane, (mats, mats)))
        before = (plane_down == plane) & (index < order)
        rank = jnp.sum(jnp.where(before, 1, 0), axis=0, keepdims=True)
        keys[1:2, :] = jnp.where(slot == 1, plane * nr + rank, -1)
    else:
        keys[1:2, :] = jnp.where(slot == 1, place, -1)

    def relay_matrices():
        member = (owner // nf) * 2 + owner % 2 + 1
        wide = half * nr
        column = lax.broadcasted_iota(jnp.int32, (wide, mats), 0) % nr
        here = jnp.where(keys[1:2, :] == z * nr + column, 1.0, 0.0).astype(BF)
        members = jnp.broadcast_to(member, (8, mats)).astype(F32).astype(BF)
        owner_of = mm(members, here, ((1,), (1,)))[0:1, :]
        line = lax.broadcasted_iota(jnp.int32, (2 * nr * blk, wide), 0)
        source = lax.broadcasted_iota(jnp.int32, (2 * nr * blk, wide), 1)
        wanted = (owner_of == (line // blk + 1).astype(F32)) & (line % blk == source // nr)
        wanted = jnp.where(wanted, 1.0, 0.0)
        spread_in[...] = wanted.astype(BF)
        spread_out[...] = jnp.transpose(wanted).astype(BF)

    few = 2 if relayed else 1

    def select(s):
        places = nz * nr if relayed and s == 1 else mats
        slot_id = lax.broadcasted_iota(jnp.int32, (places, mats), 0)
        return jnp.where(slot_id == keys[s : s + 1, :], 1.0, 0.0).astype(BF)

    def gather(s):
        chosen = select(s)

        @pl.loop(0, half // 2, unroll=half // 2 if relayed else 1)
        def _(k):
            both = jnp.concatenate([g[2 * k], g[2 * k + half], g[2 * k + 1], g[2 * k + 1 + half]], axis=0)
            out = mm(chosen, both, ((1,), (1,))).astype(BF)
            for i in range(2):
                part = out[:, 128 * i : 128 * i + 128]
                if relayed and s == 1:
                    zs_buf[:, 2 * k + i] = part.reshape(nz, nr, 128)
                else:
                    s_buf[s, :, 2 * k + i] = part.reshape(nf, nr, 128)

    def regroup_two(s, k):
        first, second = k, k + 1
        pair = jnp.concatenate(
            [s_buf[s, first].reshape(half * nr, 128), s_buf[s, second].reshape(half * nr, 128)], axis=1
        )
        out = mm(regroup[...], pair)
        t_buf[s, pl.ds(first * nr, nr)] = out[:, :128].reshape(nr, blk, 128).astype(BF)
        t_buf[s, pl.ds(second * nr, nr)] = out[:, 128:].reshape(nr, blk, 128).astype(BF)

    def regroup_all(s):
        @pl.loop(0, nf // 2, unroll=few)
        def _(k):
            regroup_two(s, 2 * k)

    def send_in(s, regrouped):
        def send(to_r, to_f):
            pltpu.make_async_remote_copy(
                t_buf.at[s, to_f * nr + to_r], v_buf.at[s, lane], in_send.at[s], in_recv.at[s],
                device_id=(to_r, to_f), device_id_type=MESH,
            ).start()

        if not regrouped:
            regroup_all(s)
        pltpu.make_async_copy(t_buf.at[s, fs * nr + rep], v_buf.at[s, lane], in_recv.at[s]).start()
        everyone(send)

    def send_out(s):
        def send(to_r, to_f):
            pltpu.make_async_remote_copy(
                w_buf.at[s, to_r * nf + lax.rem(to_f, 2) * nz + to_f // 2], u_buf.at[s, fs * nr + rep], out_send.at[s], out_recv.at[s, z],
                device_id=(to_r, to_f), device_id_type=MESH,
            ).start()

        pltpu.make_async_copy(w_buf.at[s, lane], u_buf.at[s, fs * nr + rep], out_recv.at[s, z]).start()
        everyone(send)

    def spin_momentum(s):
        wait_bytes(mom.at[s, pl.ds(0, hid)], mom_sem.at[s])
        if pad > hid:
            mom[s, hid:pad, :] = jnp.zeros((pad - hid, width), BF)

        @pl.loop(0, width // 256)
        def _(n):
            cols = tile_cols(n, 256)
            spun[s, :, cols] = mm(rows_t[...], mom[s, :, cols]).astype(BF)

    def store_momentum(s):
        own = rep * nf + fs
        mine = jnp.sum(jnp.where(owner_ref[...] == own, 1, 0), axis=1, keepdims=True)
        owned = mine > s

        @pl.loop(0, width // 256)
        def _(n):
            cols = tile_cols(n, 256)
            moment = mm(rows[0:hid, :], spun[s, :, cols])
            new[s, :, cols] = jnp.where(owned, moment, mom[s, 0:hid, cols].astype(F32)).astype(BF)

        pltpu.make_async_copy(new.at[s], new_hbm.at[s], new_sem.at[s]).start()

    def orthogonalize(s, before_last=None):
        def start(q, total):
            pair = jnp.concatenate(
                [v_buf[s, pl.ds((2 * q + i) * nf, nf)].reshape(upper, 128) for i in range(2)], axis=1
            )
            both = mm(pair, swap[...])
            cols = tile_cols(q, 128)
            for h in range(2):
                part = slice(h * upper, (h + 1) * upper)
                grad = both[:, 128 * h : 128 * h + 128]
                moment = (0.95 * spun[s, part, cols].astype(F32) + grad).astype(BF)
                spun[s, part, cols] = moment
                value = grad + 0.95 * moment.astype(F32)
                nest[part, cols] = value
                total = total + jnp.sum(value * value, axis=0, keepdims=True)
            return total

        total = lax.fori_loop(0, width // 128, start, jnp.zeros((1, 128), F32), unroll=2 * few)
        scale = 1.0 / (jnp.sqrt(jnp.sum(total, axis=1, keepdims=True)) + 1e-07)

        @pl.loop(0, width // 256, unroll=few)
        def _(n):
            cols = tile_cols(n, 256)
            x[:, cols] = (nest[:, cols] * scale).astype(BF)

        @pl.loop(0, ITERS)
        def _(turn):
            def columns(count, step):
                if relayed:
                    for n in range(count):
                        step(slice(256 * n, 256 * n + 256))
                else:
                    pl.loop(0, count)(lambda n: step(tile_cols(n, 256)))

            def to_gram(cols):
                gram[:, cols] = mm(x[...], x[cols, :], ((1,), (1,))).astype(BF)

            def to_mixed(cols):
                part = gram[:, cols]
                square = mm(gram[...], part)
                mixed[:, cols] = (-4.775 * part.astype(F32) + 2.0315 * square).astype(BF)

            def to_x(cols):
                part = x[:, cols]
                product = mm(mixed[...], part)
                x[:, cols] = (3.4445 * part.astype(F32) + product).astype(BF)

            columns(pad // 256, to_gram)
            columns(pad // 256, to_mixed)
            if before_last is not None:
                pl.when(turn == ITERS - 1)(before_last)
            columns(width // 256, to_x)

        factor = 0.2 * max(hid, width) ** 0.5

        @pl.loop(0, nr // 2, unroll=2 * few)
        def _(q):
            cols = tile_cols(q, 128)
            both = jnp.concatenate(
                [(factor * x[h * upper : (h + 1) * upper, cols].astype(F32)).astype(BF) for h in range(2)], axis=1
            )
            out = mm(both, swap[...])
            for i in range(2):
                w_buf[s, pl.ds((2 * q + i) * nf, nf)] = (
                    out[:, 128 * i : 128 * i + 128].reshape(nf, blk, 128).astype(BF)
                )

    def ungroup(s):
        def one(dz):
            k = lax.rem(z + dz, nz)
            wait_bytes(u_buf.at[s, pl.ds(2 * k * nr, 2 * nr)], out_recv.at[s, k])
            pair = jnp.concatenate(
                [u_buf[s, pl.ds((2 * k + i) * nr, nr)].reshape(nr * blk, 128) for i in range(2)], axis=1
            )
            out = mm(regroup_t[...], pair).astype(BF)
            s_buf[s, 2 * k] = out[:, :128].reshape(half, nr, 128)
            s_buf[s, 2 * k + 1] = out[:, 128:].reshape(half, nr, 128)

        @pl.loop(0, nz // 2 - 1)
        def _(k):
            one(k + 1)
            one(nz - 1 - k)

        @pl.loop(0, 2)
        def _(k):
            one(k * (nz // 2))

    def along_z(src, dst, send_sem, recv_sem):
        pltpu.make_async_copy(src.at[z], dst.at[z], recv_sem).start()

        def send(dz):
            to_z = lax.rem(z + dz, nz)
            pltpu.make_async_remote_copy(
                src.at[to_z], dst.at[z], send_sem, recv_sem,
                device_id=(rep, 2 * to_z + core), device_id_type=MESH,
            ).start()

        send(nz // 2)
        for k in range(nz // 2 - 1, 0, -1):
            send(k)
            send(nz - k)

    def in_plane(visit):
        visit(2 * rep + 1 - core, rep, 2 * z + 1 - core)

        @pl.loop(1, nr)
        def _(j):
            to_r = moved(j)
            for dc in range(2):
                to_c = lax.rem(core + dc, 2)
                visit(2 * to_r + to_c, to_r, 2 * z + to_c)

    def relay_in():
        @pl.loop(0, nz // 2, unroll=few)
        def _(k):
            pair = jnp.concatenate([zr_buf[2 * k + i].reshape(half * nr, 128) for i in range(2)], axis=1)
            out = mm(spread_in[...], pair)
            for i in range(2):
                zt_buf[:, 2 * k + i] = out[:, 128 * i : 128 * i + 128].reshape(2 * nr, blk, 128).astype(BF)

        def send(to, to_r, to_f):
            pltpu.make_async_remote_copy(
                zt_buf.at[to], v_buf.at[1, pl.ds(rep * nf + core * nz, nz)], p_send, in_recv.at[1],
                device_id=(to_r, to_f), device_id_type=MESH,
            ).start()

        pltpu.make_async_copy(
            zt_buf.at[2 * rep + core], v_buf.at[1, pl.ds(rep * nf + core * nz, nz)], in_recv.at[1]
        ).start()
        in_plane(send)

    def plane_out():
        def send(to, to_r, to_f):
            pltpu.make_async_remote_copy(
                w_buf.at[1, pl.ds(to * nz, nz)], zv_buf.at[2 * rep + core], po_send, po_recv,
                device_id=(to_r, to_f), device_id_type=MESH,
            ).start()

        pltpu.make_async_copy(w_buf.at[1, pl.ds((2 * rep + core) * nz, nz)], zv_buf.at[2 * rep + core], po_recv).start()
        in_plane(send)

    def relay_out():
        @pl.loop(0, nz // 2, unroll=few)
        def _(k):
            pair = jnp.concatenate(
                [zv_buf[:, 2 * k + i].reshape(2 * nr * blk, 128) for i in range(2)], axis=1
            )
            out = mm(spread_out[...], pair).astype(BF)
            for i in range(2):
                zs_buf[2 * k + i] = out[:, 128 * i : 128 * i + 128].reshape(half, nr, 128)

    def unpack(second):
        chosen = jnp.concatenate([select(0), select(1)], axis=0)

        @pl.loop(0, half // 2, unroll=half // 2 if relayed else 1)
        def _(k):
            tiles = [
                jnp.concatenate([s_buf[0, :, 2 * k + i].reshape(mats, 128), second(2 * k + i)], axis=0) for i in range(2)
            ]
            out = mm(jnp.concatenate(tiles, axis=1), chosen, ((0,), (0,))).astype(BF)
            for i in range(2):
                upd_ref[2 * k + i] = out[128 * i : 128 * i + 64]
                upd_ref[2 * k + i + half] = out[128 * i + 64 : 128 * i + 128]

    def all_but_one(ref):
        return ref.at[pl.ds(0, ref.shape[0] - 1)]

    loads[0].wait()
    if relayed:
        gather(1)
        pl.semaphore_wait(barrier, mats - 1)
        along_z(zs_buf, zr_buf, z_send, z_recv)
        gather(0)
        for load in loads[1:]:
            load.wait()
        regroup_all(0)
        relay_matrices()
        spin_momentum(1)
        spin_momentum(0)

        wait_bytes(zr_buf, z_recv)
        relay_in()
        send_in(0, True)
        wait_bytes(v_buf.at[1], in_recv.at[1])
        orthogonalize(1)
        plane_out()

        wait_bytes(v_buf.at[0], in_recv.at[0])

        def second_back():
            wait_bytes(zv_buf, po_recv)
            wait_bytes(all_but_one(zs_buf), z_send)
            relay_out()
            along_z(zs_buf, zu_buf, zo_send, zo_recv)

        orthogonalize(0, second_back)
        send_out(0)
        store_momentum(1)
        store_momentum(0)
        ungroup(0)
        wait_bytes(zu_buf, zo_recv)
        unpack(lambda a: zu_buf[:, a].reshape(nz * nr, 128))
        wait_bytes(all_but_one(zt_buf), p_send)
        wait_bytes(all_but_one(zv_buf), po_send)
        wait_bytes(all_but_one(zs_buf), zo_send)
    else:
        gather(0)
        for load in loads[1:]:
            load.wait()
        pl.semaphore_wait(barrier, mats - 1)
        send_in(0, False)
        gather(1)
        send_in(1, False)
        spin_momentum(0)
        spin_momentum(1)
        for s in range(2):
            wait_bytes(v_buf.at[s], in_recv.at[s])
            orthogonalize(s)
            send_out(s)
        for s in range(2):
            store_momentum(s)
        for s in range(2):
            ungroup(s)
        unpack(lambda a: s_buf[1, :, a].reshape(mats, 128))

    for s in range(2):
        wait_bytes(new.at[s], new_sem.at[s])
    for s in range(1 if relayed else 2):
        wait_bytes(all_but_one(t_buf.at[s]), in_send.at[s])
        wait_bytes(all_but_one(w_buf.at[s]), out_send.at[s])


def one_hot(rows, cols, pairs):
    out = np.zeros((rows, cols), np.float32)
    for i, j in pairs:
        out[i, j] = 1.0
    return jnp.asarray(out, BF)


def on_device(grads, momentum, owner):
    nf, nr = lax.axis_size("fsdp"), lax.axis_size("rep")
    mats, tile_rows, tile_cols = grads.shape
    half = tile_rows // 2
    hid, width = nf * tile_rows, nr * tile_cols
    blk = half + 2
    upper = nf * blk
    pad = 2 * upper
    nz = nf // 2

    regroup_pairs = [(r * blk + a, a * nr + r) for r in range(nr) for a in range(half)]
    row_pairs = [
        (tile_rows * f + half * h + a, h * upper + (f % 2 * nz + f // 2) * blk + a)
        for f in range(nf) for h in range(2) for a in range(half)
    ]
    swap_pairs = [(i * 128 + j * 64 + c, j * 128 + i * 64 + c) for i in range(2) for j in range(2) for c in range(64)]
    flip = lambda pairs: [(j, i) for i, j in pairs]
    regroup = one_hot(nr * blk, half * nr, regroup_pairs)
    regroup_t = one_hot(half * nr, nr * blk, flip(regroup_pairs))
    rows = one_hot(pad, pad, row_pairs)
    rows_t = one_hot(pad, pad, flip(row_pairs))
    swap = one_hot(256, 256, swap_pairs)

    vmem = pl.BlockSpec(memory_space=pltpu.VMEM)
    hbm = pl.BlockSpec(memory_space=pl.ANY)
    cfg = (nr, nf, half, hid, width, pad)
    turned = grads.transpose(1, 2, 0)
    tables = [regroup, regroup_t, rows, rows_t, swap]
    by_f = pltpu.VMEM((2, nf, half, nr, 128), BF)
    tiles = pltpu.VMEM((2, mats, blk, 128), BF)
    by_z = pltpu.VMEM((nz, half, nr, 128), BF)
    in_plane = pltpu.VMEM((2 * nr, nz, blk, 128), BF)
    one = pltpu.SemaphoreType.DMA(())
    relay_scratch = [
        by_z, by_z, in_plane, in_plane, by_z,
        pltpu.VMEM((2 * nr * blk, half * nr), BF),
        pltpu.VMEM((half * nr, 2 * nr * blk), BF),
        *[one for _ in range(7)],
    ]

    def run(relayed, operands):
        return pl.pallas_call(
            functools.partial(kernel, cfg, relayed),
            out_shape=(
                jax.ShapeDtypeStruct((tile_rows, tile_cols, mats), BF),
                jax.ShapeDtypeStruct(momentum.shape[1:], BF),
            ),
            in_specs=[vmem] + [hbm] * 7,
            out_specs=(vmem, hbm),
            scratch_shapes=[
                pltpu.VMEM(turned.shape, BF),
                *[pltpu.VMEM(table.shape, BF) for table in tables],
                pltpu.VMEM((2, mats), jnp.int32),
                by_f, tiles, tiles, tiles, tiles,
                pltpu.VMEM((2, pad, width), BF),
                pltpu.VMEM((2, pad, width), BF),
                pltpu.VMEM((2, hid, width), BF),
                pltpu.VMEM((pad, width), F32),
                pltpu.VMEM((pad, width), BF),
                pltpu.VMEM((pad, pad), BF),
                pltpu.VMEM((pad, pad), BF),
                pltpu.SemaphoreType.DMA((6,)),
                *[pltpu.SemaphoreType.DMA((2,)) for _ in range(5)],
                pltpu.SemaphoreType.DMA((2, nz)),
                *(relay_scratch if relayed else []),
            ],
            compiler_params=pltpu.CompilerParams(
                collective_id=1 if relayed else 0, has_side_effects=True, vmem_limit_bytes=58 * 1024 * 1024
            ),
            name="muon_relayed" if relayed else "muon_direct",
        )(*operands)

    order = jnp.arange(mats, dtype=jnp.int32)
    second = (owner[:, None] == owner[None, :]) & (order[:, None] < order[None, :])
    plane = (owner % nf) // 2
    in_each = second[None] & (plane[None, None, :] == jnp.arange(nz, dtype=jnp.int32)[:, None, None])
    fits = jnp.max(jnp.sum(in_each.astype(jnp.int32), axis=(1, 2))) <= nr
    operands = (owner[None, :], turned, momentum[0], *tables)
    update, new = lax.cond(fits, functools.partial(run, True), functools.partial(run, False), operands)
    return (update.transpose(2, 0, 1), new[None])


def solution(mesh):
    return jax.shard_map(
        on_device,
        mesh=mesh,
        in_specs=(P(None, "fsdp", "rep"), P(("rep", "fsdp"), None, None, None), P()),
        out_specs=(P(None, "fsdp", "rep"), P(("rep", "fsdp"), None, None, None)),
        check_vma=False,
    )
```

```python
import functools

import jax
import jax.numpy as jnp
import numpy as np
from jax import lax
from jax.experimental import pallas as pl
from jax.experimental.pallas import tpu as pltpu
from jax.sharding import PartitionSpec as P

ITERS = 2
MESH = pl.DeviceIdType.MESH
BF = jnp.bfloat16
F32 = jnp.float32


def mm(a, b, dims=((1,), (0,))):
    return lax.dot_general(a, b, (dims, ((), ())), preferred_element_type=F32)


def wait_bytes(ref, sem):
    pltpu.make_async_copy(ref, ref, sem).wait()


def tile_cols(n, size):
    return pl.ds(pl.multiple_of(n * size, size), size)


def kernel(
    cfg, relayed,
    owner_ref, g_hbm, mom_hbm, regroup_hbm, regroup_t_hbm, rows_hbm, rows_t_hbm, swap_hbm,
    upd_ref, new_hbm,
    g, regroup, regroup_t, rows, rows_t, swap, keys,
    s_buf, t_buf, v_buf, w_buf, u_buf, mom, spun, new, nest, x, gram, mixed,
    load_sem, mom_sem, new_sem, in_send, in_recv, out_send, out_recv,
    *relay_refs,
):
    nr, nf, half, hid, width, pad = cfg
    rep, fs = lax.axis_index("rep"), lax.axis_index("fsdp")
    mats = nr * nf
    blk = half + 2
    upper = nf * blk
    nz = nf // 2
    z, core = fs // 2, lax.rem(fs, 2)
    lane = rep * nf + core * nz + z
    if relayed:
        (zs_buf, zr_buf, zt_buf, zv_buf, zu_buf, spread_in, spread_out,
         z_send, z_recv, p_send, zo_send, zo_recv, po_send, po_recv) = relay_refs

    loads = [(g_hbm, g), (regroup_hbm, regroup), (swap_hbm, swap), (rows_hbm, rows),
             (rows_t_hbm, rows_t), (regroup_t_hbm, regroup_t)]
    loads = [pltpu.make_async_copy(a, b, load_sem.at[i]) for i, (a, b) in enumerate(loads)]
    for load in loads:
        load.start()
    for s in range(2):
        pltpu.make_async_copy(mom_hbm.at[s], mom.at[s, pl.ds(0, hid)], mom_sem.at[s]).start()

    side = 4
    rx, ry = rep // side, lax.rem(rep, side)

    def moved(j):
        return lax.rem(rx + j, side) * side + lax.rem(ry + j // side + j, side)

    def faces(dz, dc):
        return 2 * lax.rem(z + dz, nz) + lax.rem(core + dc, 2)

    def everyone(visit, beside=None):
        def four(k, j):
            to_r = moved(j)
            for dc in range(2):
                visit(to_r, faces(k + 1, dc))
                visit(to_r, faces(nz - 1 - k, dc))

        done = 0
        if beside is not None:
            done = 2
            for k in range(done):
                @pl.loop(0, nr)
                def _(j):
                    beside(k * nr + j)
                    four(k, j)

        @pl.loop(done, nz // 2 - 1)
        def _(k):
            @pl.loop(0, nr)
            def _(j):
                four(k, j)

        for dc in range(2):
            visit(rep, faces(nz // 2, dc))
        visit(rep, faces(0, 1))

        @pl.loop(1, nr)
        def _(j):
            to_r = moved(j)
            for dc in range(2):
                visit(to_r, faces(nz // 2, dc))
                visit(to_r, faces(0, dc))

    barrier = pltpu.get_barrier_semaphore()

    def greet(to_r, to_f):
        pl.semaphore_signal(barrier, inc=1, device_id=(to_r, to_f), device_id_type=MESH)

    everyone(greet)

    owner = owner_ref[...]
    down = jnp.transpose(jnp.broadcast_to(owner, (mats, mats)))
    index = lax.broadcasted_iota(jnp.int32, (mats, mats), 0)
    order = lax.broadcasted_iota(jnp.int32, (mats, mats), 1)
    earlier = (down == owner) & (index < order)
    slot = jnp.sum(jnp.where(earlier, 1, 0), axis=0, keepdims=True)
    place = (owner % nf) * nr + owner // nf
    keys[0:1, :] = jnp.where(slot == 0, place, -1)
    if relayed:
        plane = jnp.where(slot == 1, (owner % nf) // 2, -1)
        plane_down = jnp.transpose(jnp.broadcast_to(plane, (mats, mats)))
        before = (plane_down == plane) & (index < order)
        rank = jnp.sum(jnp.where(before, 1, 0), axis=0, keepdims=True)
        keys[1:2, :] = jnp.where(slot == 1, plane * nr + rank, -1)
    else:
        keys[1:2, :] = jnp.where(slot == 1, place, -1)

    def relay_matrices():
        member = (owner // nf) * 2 + owner % 2 + 1
        wide = half * nr
        column = lax.broadcasted_iota(jnp.int32, (wide, mats), 0) % nr
        here = jnp.where(keys[1:2, :] == z * nr + column, 1.0, 0.0).astype(BF)
        members = jnp.broadcast_to(member, (8, mats)).astype(F32).astype(BF)
        owner_of = mm(members, here, ((1,), (1,)))[0:1, :]
        line = lax.broadcasted_iota(jnp.int32, (2 * nr * blk, wide), 0)
        source = lax.broadcasted_iota(jnp.int32, (2 * nr * blk, wide), 1)
        wanted = (owner_of == (line // blk + 1).astype(F32)) & (line % blk == source // nr)
        wanted = jnp.where(wanted, 1.0, 0.0)
        spread_in[...] = wanted.astype(BF)
        spread_out[...] = jnp.transpose(wanted).astype(BF)

    few = 2 if relayed else 1

    def select(s):
        places = nz * nr if relayed and s == 1 else mats
        slot_id = lax.broadcasted_iota(jnp.int32, (places, mats), 0)
        return jnp.where(slot_id == keys[s : s + 1, :], 1.0, 0.0).astype(BF)

    def gather(s):
        chosen = select(s)

        @pl.loop(0, half // 2, unroll=half // 2 if relayed else 1)
        def _(k):
            both = jnp.concatenate([g[2 * k], g[2 * k + half], g[2 * k + 1], g[2 * k + 1 + half]], axis=0)
            out = mm(chosen, both, ((1,), (1,))).astype(BF)
            for i in range(2):
                part = out[:, 128 * i : 128 * i + 128]
                if relayed and s == 1:
                    zs_buf[:, 2 * k + i] = part.reshape(nz, nr, 128)
                else:
                    s_buf[s, :, 2 * k + i] = part.reshape(nf, nr, 128)

    def regroup_two(s, k):
        first, second = k, k + 1
        pair = jnp.concatenate(
            [s_buf[s, first].reshape(half * nr, 128), s_buf[s, second].reshape(half * nr, 128)], axis=1
        )
        out = mm(regroup[...], pair)
        t_buf[s, pl.ds(first * nr, nr)] = out[:, :128].reshape(nr, blk, 128).astype(BF)
        t_buf[s, pl.ds(second * nr, nr)] = out[:, 128:].reshape(nr, blk, 128).astype(BF)

    def regroup_all(s):
        @pl.loop(0, nf // 2, unroll=few)
        def _(k):
            regroup_two(s, 2 * k)

    def send_in(s, regrouped, beside=None):
        def send(to_r, to_f):
            pltpu.make_async_remote_copy(
                t_buf.at[s, to_f * nr + to_r], v_buf.at[s, lane], in_send.at[s], in_recv.at[s],
                device_id=(to_r, to_f), device_id_type=MESH,
            ).start()

        if not regrouped:
            regroup_all(s)
        pltpu.make_async_copy(t_buf.at[s, fs * nr + rep], v_buf.at[s, lane], in_recv.at[s]).start()
        everyone(send, beside)

    def send_out(s):
        def send(to_r, to_f):
            pltpu.make_async_remote_copy(
                w_buf.at[s, to_r * nf + lax.rem(to_f, 2) * nz + to_f // 2], u_buf.at[s, fs * nr + rep], out_send.at[s], out_recv.at[s, z],
                device_id=(to_r, to_f), device_id_type=MESH,
            ).start()

        pltpu.make_async_copy(w_buf.at[s, lane], u_buf.at[s, fs * nr + rep], out_recv.at[s, z]).start()
        everyone(send)

    def spin_momentum(s):
        wait_bytes(mom.at[s, pl.ds(0, hid)], mom_sem.at[s])
        if pad > hid:
            mom[s, hid:pad, :] = jnp.zeros((pad - hid, width), BF)

        @pl.loop(0, width // 256)
        def _(n):
            cols = tile_cols(n, 256)
            spun[s, :, cols] = mm(rows_t[...], mom[s, :, cols]).astype(BF)

    def store_momentum(s):
        own = rep * nf + fs
        mine = jnp.sum(jnp.where(owner_ref[...] == own, 1, 0), axis=1, keepdims=True)
        owned = mine > s

        @pl.loop(0, width // 256)
        def _(n):
            cols = tile_cols(n, 256)
            moment = mm(rows[0:hid, :], spun[s, :, cols])
            new[s, :, cols] = jnp.where(owned, moment, mom[s, 0:hid, cols].astype(F32)).astype(BF)

        pltpu.make_async_copy(new.at[s], new_hbm.at[s], new_sem.at[s]).start()

    def orthogonalize(s):
        def start(q, total):
            pair = jnp.concatenate(
                [v_buf[s, pl.ds((2 * q + i) * nf, nf)].reshape(upper, 128) for i in range(2)], axis=1
            )
            both = mm(pair, swap[...])
            cols = tile_cols(q, 128)
            for h in range(2):
                part = slice(h * upper, (h + 1) * upper)
                grad = both[:, 128 * h : 128 * h + 128]
                moment = (0.95 * spun[s, part, cols].astype(F32) + grad).astype(BF)
                spun[s, part, cols] = moment
                value = grad + 0.95 * moment.astype(F32)
                nest[part, cols] = value
                total = total + jnp.sum(value * value, axis=0, keepdims=True)
            return total

        total = lax.fori_loop(0, width // 128, start, jnp.zeros((1, 128), F32), unroll=2 * few)
        scale = 1.0 / (jnp.sqrt(jnp.sum(total, axis=1, keepdims=True)) + 1e-07)

        @pl.loop(0, width // 256, unroll=few)
        def _(n):
            cols = tile_cols(n, 256)
            x[:, cols] = (nest[:, cols] * scale).astype(BF)

        @pl.loop(0, ITERS)
        def _(turn):
            def columns(count, step):
                if relayed:
                    for n in range(count):
                        step(slice(256 * n, 256 * n + 256))
                else:
                    pl.loop(0, count)(lambda n: step(tile_cols(n, 256)))

            def to_gram(cols):
                gram[:, cols] = mm(x[...], x[cols, :], ((1,), (1,))).astype(BF)

            def to_mixed(cols):
                part = gram[:, cols]
                square = mm(gram[...], part)
                mixed[:, cols] = (-4.775 * part.astype(F32) + 2.0315 * square).astype(BF)

            def to_x(cols):
                part = x[:, cols]
                product = mm(mixed[...], part)
                x[:, cols] = (3.4445 * part.astype(F32) + product).astype(BF)

            columns(pad // 256, to_gram)
            columns(pad // 256, to_mixed)
            columns(width // 256, to_x)

        factor = 0.2 * max(hid, width) ** 0.5

        @pl.loop(0, nr // 2, unroll=2 * few)
        def _(q):
            cols = tile_cols(q, 128)
            both = jnp.concatenate(
                [(factor * x[h * upper : (h + 1) * upper, cols].astype(F32)).astype(BF) for h in range(2)], axis=1
            )
            out = mm(both, swap[...])
            for i in range(2):
                w_buf[s, pl.ds((2 * q + i) * nf, nf)] = (
                    out[:, 128 * i : 128 * i + 128].reshape(nf, blk, 128).astype(BF)
                )

    def ungroup(s):
        def one(dz):
            k = lax.rem(z + dz, nz)
            wait_bytes(u_buf.at[s, pl.ds(2 * k * nr, 2 * nr)], out_recv.at[s, k])
            pair = jnp.concatenate(
                [u_buf[s, pl.ds((2 * k + i) * nr, nr)].reshape(nr * blk, 128) for i in range(2)], axis=1
            )
            out = mm(regroup_t[...], pair).astype(BF)
            s_buf[s, 2 * k] = out[:, :128].reshape(half, nr, 128)
            s_buf[s, 2 * k + 1] = out[:, 128:].reshape(half, nr, 128)

        @pl.loop(0, nz // 2 - 1)
        def _(k):
            one(k + 1)
            one(nz - 1 - k)

        @pl.loop(0, 2)
        def _(k):
            one(k * (nz // 2))

    def along_z(src, dst, send_sem, recv_sem):
        pltpu.make_async_copy(src.at[z], dst.at[z], recv_sem).start()

        def send(dz):
            to_z = lax.rem(z + dz, nz)
            pltpu.make_async_remote_copy(
                src.at[to_z], dst.at[z], send_sem, recv_sem,
                device_id=(rep, 2 * to_z + core), device_id_type=MESH,
            ).start()

        send(nz // 2)
        for k in range(nz // 2 - 1, 0, -1):
            send(k)
            send(nz - k)

    def in_plane(visit):
        visit(2 * rep + 1 - core, rep, 2 * z + 1 - core)

        @pl.loop(1, nr)
        def _(j):
            to_r = moved(j)
            for dc in range(2):
                to_c = lax.rem(core + dc, 2)
                visit(2 * to_r + to_c, to_r, 2 * z + to_c)

    def relay_in():
        @pl.loop(0, nz // 2, unroll=few)
        def _(k):
            pair = jnp.concatenate([zr_buf[2 * k + i].reshape(half * nr, 128) for i in range(2)], axis=1)
            out = mm(spread_in[...], pair)
            for i in range(2):
                zt_buf[:, 2 * k + i] = out[:, 128 * i : 128 * i + 128].reshape(2 * nr, blk, 128).astype(BF)

    def send_in_plane(t):
        to_r = moved(t // 2)
        to_c = lax.rem(core + t, 2)

        @pl.when(t > 0)
        def _():
            pltpu.make_async_remote_copy(
                zt_buf.at[2 * to_r + to_c], v_buf.at[1, pl.ds(rep * nf + core * nz, nz)], p_send, in_recv.at[1],
                device_id=(to_r, 2 * z + to_c), device_id_type=MESH,
            ).start()

        @pl.when(t == 0)
        def _():
            pltpu.make_async_copy(
                zt_buf.at[2 * rep + core], v_buf.at[1, pl.ds(rep * nf + core * nz, nz)], in_recv.at[1]
            ).start()

    def plane_out():
        def send(to, to_r, to_f):
            pltpu.make_async_remote_copy(
                w_buf.at[1, pl.ds(to * nz, nz)], zv_buf.at[2 * rep + core], po_send, po_recv,
                device_id=(to_r, to_f), device_id_type=MESH,
            ).start()

        pltpu.make_async_copy(w_buf.at[1, pl.ds((2 * rep + core) * nz, nz)], zv_buf.at[2 * rep + core], po_recv).start()
        in_plane(send)

    def relay_out():
        @pl.loop(0, nz // 2, unroll=few)
        def _(k):
            pair = jnp.concatenate(
                [zv_buf[:, 2 * k + i].reshape(2 * nr * blk, 128) for i in range(2)], axis=1
            )
            out = mm(spread_out[...], pair).astype(BF)
            for i in range(2):
                zs_buf[2 * k + i] = out[:, 128 * i : 128 * i + 128].reshape(half, nr, 128)

    def unpack(second):
        chosen = jnp.concatenate([select(0), select(1)], axis=0)

        @pl.loop(0, half // 2, unroll=half // 2 if relayed else 1)
        def _(k):
            tiles = [
                jnp.concatenate([s_buf[0, :, 2 * k + i].reshape(mats, 128), second(2 * k + i)], axis=0) for i in range(2)
            ]
            out = mm(jnp.concatenate(tiles, axis=1), chosen, ((0,), (0,))).astype(BF)
            for i in range(2):
                upd_ref[2 * k + i] = out[128 * i : 128 * i + 64]
                upd_ref[2 * k + i + half] = out[128 * i + 64 : 128 * i + 128]

    def all_but_one(ref):
        return ref.at[pl.ds(0, ref.shape[0] - 1)]

    loads[0].wait()
    if relayed:
        gather(1)
        pl.semaphore_wait(barrier, mats - 1)
        along_z(zs_buf, zr_buf, z_send, z_recv)
        gather(0)
        for load in loads[1:]:
            load.wait()
        regroup_all(0)
        relay_matrices()
        spin_momentum(1)
        spin_momentum(0)

        wait_bytes(zr_buf, z_recv)
        relay_in()
        send_in(0, True, send_in_plane)
        wait_bytes(v_buf.at[1], in_recv.at[1])
        orthogonalize(1)
        plane_out()

        wait_bytes(v_buf.at[0], in_recv.at[0])
        orthogonalize(0)
        send_out(0)

        wait_bytes(zv_buf, po_recv)
        wait_bytes(all_but_one(zs_buf), z_send)
        relay_out()
        along_z(zs_buf, zu_buf, zo_send, zo_recv)
        store_momentum(1)
        store_momentum(0)

        ungroup(0)
        wait_bytes(zu_buf, zo_recv)
        unpack(lambda a: zu_buf[:, a].reshape(nz * nr, 128))
        wait_bytes(all_but_one(zt_buf), p_send)
        wait_bytes(all_but_one(zv_buf), po_send)
        wait_bytes(all_but_one(zs_buf), zo_send)
    else:
        gather(0)
        for load in loads[1:]:
            load.wait()
        pl.semaphore_wait(barrier, mats - 1)
        send_in(0, False)
        gather(1)
        send_in(1, False)
        spin_momentum(0)
        spin_momentum(1)
        for s in range(2):
            wait_bytes(v_buf.at[s], in_recv.at[s])
            orthogonalize(s)
            send_out(s)
        for s in range(2):
            store_momentum(s)
        for s in range(2):
            ungroup(s)
        unpack(lambda a: s_buf[1, :, a].reshape(mats, 128))

    for s in range(2):
        wait_bytes(new.at[s], new_sem.at[s])
    for s in range(1 if relayed else 2):
        wait_bytes(all_but_one(t_buf.at[s]), in_send.at[s])
        wait_bytes(all_but_one(w_buf.at[s]), out_send.at[s])


def one_hot(rows, cols, pairs):
    out = np.zeros((rows, cols), np.float32)
    for i, j in pairs:
        out[i, j] = 1.0
    return jnp.asarray(out, BF)


def on_device(grads, momentum, owner):
    nf, nr = lax.axis_size("fsdp"), lax.axis_size("rep")
    mats, tile_rows, tile_cols = grads.shape
    half = tile_rows // 2
    hid, width = nf * tile_rows, nr * tile_cols
    blk = half + 2
    upper = nf * blk
    pad = 2 * upper
    nz = nf // 2

    regroup_pairs = [(r * blk + a, a * nr + r) for r in range(nr) for a in range(half)]
    row_pairs = [
        (tile_rows * f + half * h + a, h * upper + (f % 2 * nz + f // 2) * blk + a)
        for f in range(nf) for h in range(2) for a in range(half)
    ]
    swap_pairs = [(i * 128 + j * 64 + c, j * 128 + i * 64 + c) for i in range(2) for j in range(2) for c in range(64)]
    flip = lambda pairs: [(j, i) for i, j in pairs]
    regroup = one_hot(nr * blk, half * nr, regroup_pairs)
    regroup_t = one_hot(half * nr, nr * blk, flip(regroup_pairs))
    rows = one_hot(pad, pad, row_pairs)
    rows_t = one_hot(pad, pad, flip(row_pairs))
    swap = one_hot(256, 256, swap_pairs)

    vmem = pl.BlockSpec(memory_space=pltpu.VMEM)
    hbm = pl.BlockSpec(memory_space=pl.ANY)
    cfg = (nr, nf, half, hid, width, pad)
    turned = grads.transpose(1, 2, 0)
    tables = [regroup, regroup_t, rows, rows_t, swap]
    by_f = pltpu.VMEM((2, nf, half, nr, 128), BF)
    tiles = pltpu.VMEM((2, mats, blk, 128), BF)
    by_z = pltpu.VMEM((nz, half, nr, 128), BF)
    in_plane = pltpu.VMEM((2 * nr, nz, blk, 128), BF)
    one = pltpu.SemaphoreType.DMA(())
    relay_scratch = [
        by_z, by_z, in_plane, in_plane, by_z,
        pltpu.VMEM((2 * nr * blk, half * nr), BF),
        pltpu.VMEM((half * nr, 2 * nr * blk), BF),
        *[one for _ in range(7)],
    ]

    def run(relayed, operands):
        return pl.pallas_call(
            functools.partial(kernel, cfg, relayed),
            out_shape=(
                jax.ShapeDtypeStruct((tile_rows, tile_cols, mats), BF),
                jax.ShapeDtypeStruct(momentum.shape[1:], BF),
            ),
            in_specs=[vmem] + [hbm] * 7,
            out_specs=(vmem, hbm),
            scratch_shapes=[
                pltpu.VMEM(turned.shape, BF),
                *[pltpu.VMEM(table.shape, BF) for table in tables],
                pltpu.VMEM((2, mats), jnp.int32),
                by_f, tiles, tiles, tiles, tiles,
                pltpu.VMEM((2, pad, width), BF),
                pltpu.VMEM((2, pad, width), BF),
                pltpu.VMEM((2, hid, width), BF),
                pltpu.VMEM((pad, width), F32),
                pltpu.VMEM((pad, width), BF),
                pltpu.VMEM((pad, pad), BF),
                pltpu.VMEM((pad, pad), BF),
                pltpu.SemaphoreType.DMA((6,)),
                *[pltpu.SemaphoreType.DMA((2,)) for _ in range(5)],
                pltpu.SemaphoreType.DMA((2, nz)),
                *(relay_scratch if relayed else []),
            ],
            compiler_params=pltpu.CompilerParams(
                collective_id=1 if relayed else 0, has_side_effects=True, vmem_limit_bytes=58 * 1024 * 1024
            ),
            name="muon_relayed" if relayed else "muon_direct",
        )(*operands)

    order = jnp.arange(mats, dtype=jnp.int32)
    second = (owner[:, None] == owner[None, :]) & (order[:, None] < order[None, :])
    plane = (owner % nf) // 2
    in_each = second[None] & (plane[None, None, :] == jnp.arange(nz, dtype=jnp.int32)[:, None, None])
    fits = jnp.max(jnp.sum(in_each.astype(jnp.int32), axis=(1, 2))) <= nr
    operands = (owner[None, :], turned, momentum[0], *tables)
    update, new = lax.cond(fits, functools.partial(run, True), functools.partial(run, False), operands)
    return (update.transpose(2, 0, 1), new[None])


def solution(mesh):
    return jax.shard_map(
        on_device,
        mesh=mesh,
        in_specs=(P(None, "fsdp", "rep"), P(("rep", "fsdp"), None, None, None), P()),
        out_specs=(P(None, "fsdp", "rep"), P(("rep", "fsdp"), None, None, None)),
        check_vma=False,
    )
```

```python
import functools

import jax
import jax.numpy as jnp
import numpy as np
from jax import lax
from jax.experimental import pallas as pl
from jax.experimental.pallas import tpu as pltpu
from jax.sharding import PartitionSpec as P

ITERS = 2
MESH = pl.DeviceIdType.MESH
BF = jnp.bfloat16
F32 = jnp.float32


def mm(a, b, dims=((1,), (0,))):
    return lax.dot_general(a, b, (dims, ((), ())), preferred_element_type=F32)


def wait_bytes(ref, sem):
    pltpu.make_async_copy(ref, ref, sem).wait()


def tile_cols(n, size):
    return pl.ds(pl.multiple_of(n * size, size), size)


def kernel(
    cfg, relayed,
    owner_ref, g_hbm, mom_hbm, regroup_hbm, regroup_t_hbm, rows_hbm, rows_t_hbm, swap_hbm,
    upd_ref, new_hbm,
    g, regroup, regroup_t, rows, rows_t, swap, keys,
    s_buf, t_buf, v_buf, w_buf, u_buf, mom, spun, new, nest, x, gram, mixed,
    load_sem, mom_sem, new_sem, in_send, in_recv, out_send, out_recv,
    *relay_refs,
):
    nr, nf, half, hid, width, pad = cfg
    rep, fs = lax.axis_index("rep"), lax.axis_index("fsdp")
    mats = nr * nf
    blk = half + 2
    upper = nf * blk
    nz = nf // 2
    z, core = fs // 2, lax.rem(fs, 2)
    lane = rep * nf + core * nz + z
    if relayed:
        (zs_buf, zr_buf, zt_buf, zv_buf, zu_buf, spread_in, spread_out,
         z_send, z_recv, p_send, zo_send, zo_recv, po_send, po_recv) = relay_refs

    loads = [(g_hbm, g), (regroup_hbm, regroup), (swap_hbm, swap), (rows_hbm, rows),
             (rows_t_hbm, rows_t), (regroup_t_hbm, regroup_t)]
    loads = [pltpu.make_async_copy(a, b, load_sem.at[i]) for i, (a, b) in enumerate(loads)]
    for load in loads:
        load.start()
    for s in range(2):
        pltpu.make_async_copy(mom_hbm.at[s], mom.at[s, pl.ds(0, hid)], mom_sem.at[s]).start()

    side = 4
    rx, ry = rep // side, lax.rem(rep, side)

    def moved(j):
        return lax.rem(rx + j, side) * side + lax.rem(ry + j // side + j, side)

    def faces(dz, dc):
        return 2 * lax.rem(z + dz, nz) + lax.rem(core + dc, 2)

    def everyone(visit):
        def four(k, j):
            to_r = moved(j)
            for dc in range(2):
                visit(to_r, faces(k + 1, dc))
                visit(to_r, faces(nz - 1 - k, dc))

        @pl.loop(0, nz // 2 - 1)
        def _(k):
            @pl.loop(0, nr)
            def _(j):
                four(k, j)

        for dc in range(2):
            visit(rep, faces(nz // 2, dc))
        visit(rep, faces(0, 1))

        @pl.loop(1, nr)
        def _(j):
            to_r = moved(j)
            for dc in range(2):
                visit(to_r, faces(nz // 2, dc))
                visit(to_r, faces(0, dc))

    barrier = pltpu.get_barrier_semaphore()

    def greet(to_r, to_f):
        pl.semaphore_signal(barrier, inc=1, device_id=(to_r, to_f), device_id_type=MESH)

    everyone(greet)

    owner = owner_ref[...]
    down = jnp.transpose(jnp.broadcast_to(owner, (mats, mats)))
    index = lax.broadcasted_iota(jnp.int32, (mats, mats), 0)
    order = lax.broadcasted_iota(jnp.int32, (mats, mats), 1)
    earlier = (down == owner) & (index < order)
    slot = jnp.sum(jnp.where(earlier, 1, 0), axis=0, keepdims=True)
    place = (owner % nf) * nr + owner // nf
    keys[0:1, :] = jnp.where(slot == 0, place, -1)
    if relayed:
        plane = jnp.where(slot == 1, (owner % nf) // 2, -1)
        plane_down = jnp.transpose(jnp.broadcast_to(plane, (mats, mats)))
        before = (plane_down == plane) & (index < order)
        rank = jnp.sum(jnp.where(before, 1, 0), axis=0, keepdims=True)
        keys[1:2, :] = jnp.where(slot == 1, plane * nr + rank, -1)
    else:
        keys[1:2, :] = jnp.where(slot == 1, place, -1)

    def relay_matrices():
        member = (owner // nf) * 2 + owner % 2 + 1
        wide = half * nr
        column = lax.broadcasted_iota(jnp.int32, (wide, mats), 0) % nr
        here = jnp.where(keys[1:2, :] == z * nr + column, 1.0, 0.0).astype(BF)
        members = jnp.broadcast_to(member, (8, mats)).astype(F32).astype(BF)
        owner_of = mm(members, here, ((1,), (1,)))[0:1, :]
        line = lax.broadcasted_iota(jnp.int32, (2 * nr * blk, wide), 0)
        source = lax.broadcasted_iota(jnp.int32, (2 * nr * blk, wide), 1)
        wanted = (owner_of == (line // blk + 1).astype(F32)) & (line % blk == source // nr)
        wanted = jnp.where(wanted, 1.0, 0.0)
        spread_in[...] = wanted.astype(BF)
        spread_out[...] = jnp.transpose(wanted).astype(BF)

    few = 2 if relayed else 1

    def select(s):
        places = nz * nr if relayed and s == 1 else mats
        slot_id = lax.broadcasted_iota(jnp.int32, (places, mats), 0)
        return jnp.where(slot_id == keys[s : s + 1, :], 1.0, 0.0).astype(BF)

    def gather(s):
        chosen = select(s)

        @pl.loop(0, half // 2, unroll=half // 2 if relayed else 1)
        def _(k):
            both = jnp.concatenate([g[2 * k], g[2 * k + half], g[2 * k + 1], g[2 * k + 1 + half]], axis=0)
            out = mm(chosen, both, ((1,), (1,))).astype(BF)
            for i in range(2):
                part = out[:, 128 * i : 128 * i + 128]
                if relayed and s == 1:
                    zs_buf[:, 2 * k + i] = part.reshape(nz, nr, 128)
                else:
                    s_buf[s, :, 2 * k + i] = part.reshape(nf, nr, 128)

    def regroup_two(s, k):
        first, second = k, k + 1
        pair = jnp.concatenate(
            [s_buf[s, first].reshape(half * nr, 128), s_buf[s, second].reshape(half * nr, 128)], axis=1
        )
        out = mm(regroup[...], pair)
        t_buf[s, pl.ds(first * nr, nr)] = out[:, :128].reshape(nr, blk, 128).astype(BF)
        t_buf[s, pl.ds(second * nr, nr)] = out[:, 128:].reshape(nr, blk, 128).astype(BF)

    def regroup_all(s):
        @pl.loop(0, nf // 2, unroll=few)
        def _(k):
            regroup_two(s, 2 * k)

    def send_in(s, regrouped):
        def send(to_r, to_f):
            pltpu.make_async_remote_copy(
                t_buf.at[s, to_f * nr + to_r], v_buf.at[s, lane], in_send.at[s], in_recv.at[s],
                device_id=(to_r, to_f), device_id_type=MESH,
            ).start()

        if not regrouped:
            regroup_all(s)
        pltpu.make_async_copy(t_buf.at[s, fs * nr + rep], v_buf.at[s, lane], in_recv.at[s]).start()
        everyone(send)

    def send_out(s):
        def send(to_r, to_f):
            pltpu.make_async_remote_copy(
                w_buf.at[s, to_r * nf + lax.rem(to_f, 2) * nz + to_f // 2], u_buf.at[s, fs * nr + rep], out_send.at[s], out_recv.at[s, z],
                device_id=(to_r, to_f), device_id_type=MESH,
            ).start()

        pltpu.make_async_copy(w_buf.at[s, lane], u_buf.at[s, fs * nr + rep], out_recv.at[s, z]).start()
        everyone(send)

    def spin_momentum(s):
        wait_bytes(mom.at[s, pl.ds(0, hid)], mom_sem.at[s])
        if pad > hid:
            mom[s, hid:pad, :] = jnp.zeros((pad - hid, width), BF)

        @pl.loop(0, width // 256)
        def _(n):
            cols = tile_cols(n, 256)
            spun[s, :, cols] = mm(rows_t[...], mom[s, :, cols]).astype(BF)

    def store_momentum(s):
        own = rep * nf + fs
        mine = jnp.sum(jnp.where(owner_ref[...] == own, 1, 0), axis=1, keepdims=True)
        owned = mine > s

        @pl.loop(0, width // 256)
        def _(n):
            cols = tile_cols(n, 256)
            moment = mm(rows[0:hid, :], spun[s, :, cols])
            new[s, :, cols] = jnp.where(owned, moment, mom[s, 0:hid, cols].astype(F32)).astype(BF)

        pltpu.make_async_copy(new.at[s], new_hbm.at[s], new_sem.at[s]).start()

    def orthogonalize(s):
        def start(q, total):
            pair = jnp.concatenate(
                [v_buf[s, pl.ds((2 * q + i) * nf, nf)].reshape(upper, 128) for i in range(2)], axis=1
            )
            both = mm(pair, swap[...])
            cols = tile_cols(q, 128)
            for h in range(2):
                part = slice(h * upper, (h + 1) * upper)
                grad = both[:, 128 * h : 128 * h + 128]
                moment = (0.95 * spun[s, part, cols].astype(F32) + grad).astype(BF)
                spun[s, part, cols] = moment
                value = grad + 0.95 * moment.astype(F32)
                nest[part, cols] = value
                total = total + jnp.sum(value * value, axis=0, keepdims=True)
            return total

        total = lax.fori_loop(0, width // 128, start, jnp.zeros((1, 128), F32), unroll=2 * few)
        scale = 1.0 / (jnp.sqrt(jnp.sum(total, axis=1, keepdims=True)) + 1e-07)

        @pl.loop(0, width // 256, unroll=few)
        def _(n):
            cols = tile_cols(n, 256)
            x[:, cols] = (nest[:, cols] * scale).astype(BF)

        @pl.loop(0, ITERS)
        def _(turn):
            def columns(count, step):
                if relayed:
                    for n in range(count):
                        step(slice(256 * n, 256 * n + 256))
                else:
                    pl.loop(0, count)(lambda n: step(tile_cols(n, 256)))

            def mirror(ref, cols, part):
                lines = slice(cols.start, pad)
                ref[lines, cols] = part.astype(BF)
                if cols.stop < pad:
                    ref[cols, cols.stop : pad] = jnp.transpose(part[256:]).astype(BF)

            def to_gram(cols):
                if relayed:
                    mirror(gram, cols, mm(x[cols.start :, :], x[cols, :], ((1,), (1,))))
                else:
                    gram[:, cols] = mm(x[...], x[cols, :], ((1,), (1,))).astype(BF)

            def to_mixed(cols):
                lines = slice(cols.start if relayed else 0, pad)
                part = -4.775 * gram[lines, cols].astype(F32) + 2.0315 * mm(gram[lines, :], gram[:, cols])
                if relayed:
                    mirror(mixed, cols, part)
                else:
                    mixed[:, cols] = part.astype(BF)

            def to_x(cols):
                part = x[:, cols]
                product = mm(mixed[...], part)
                x[:, cols] = (3.4445 * part.astype(F32) + product).astype(BF)

            columns(pad // 256, to_gram)
            columns(pad // 256, to_mixed)
            columns(width // 256, to_x)

        factor = 0.2 * max(hid, width) ** 0.5

        @pl.loop(0, nr // 2, unroll=2 * few)
        def _(q):
            cols = tile_cols(q, 128)
            both = jnp.concatenate(
                [(factor * x[h * upper : (h + 1) * upper, cols].astype(F32)).astype(BF) for h in range(2)], axis=1
            )
            out = mm(both, swap[...])
            for i in range(2):
                w_buf[s, pl.ds((2 * q + i) * nf, nf)] = (
                    out[:, 128 * i : 128 * i + 128].reshape(nf, blk, 128).astype(BF)
                )

    def ungroup(s):
        def one(dz):
            k = lax.rem(z + dz, nz)
            wait_bytes(u_buf.at[s, pl.ds(2 * k * nr, 2 * nr)], out_recv.at[s, k])
            pair = jnp.concatenate(
                [u_buf[s, pl.ds((2 * k + i) * nr, nr)].reshape(nr * blk, 128) for i in range(2)], axis=1
            )
            out = mm(regroup_t[...], pair).astype(BF)
            s_buf[s, 2 * k] = out[:, :128].reshape(half, nr, 128)
            s_buf[s, 2 * k + 1] = out[:, 128:].reshape(half, nr, 128)

        @pl.loop(0, nz // 2 - 1)
        def _(k):
            one(k + 1)
            one(nz - 1 - k)

        @pl.loop(0, 2)
        def _(k):
            one(k * (nz // 2))

    def along_z(src, dst, send_sem, recv_sem):
        pltpu.make_async_copy(src.at[z], dst.at[z], recv_sem).start()

        def send(dz):
            to_z = lax.rem(z + dz, nz)
            pltpu.make_async_remote_copy(
                src.at[to_z], dst.at[z], send_sem, recv_sem,
                device_id=(rep, 2 * to_z + core), device_id_type=MESH,
            ).start()

        send(nz // 2)
        for k in range(nz // 2 - 1, 0, -1):
            send(k)
            send(nz - k)

    def in_plane(visit):
        visit(2 * rep + 1 - core, rep, 2 * z + 1 - core)

        @pl.loop(1, nr)
        def _(j):
            to_r = moved(j)
            for dc in range(2):
                to_c = lax.rem(core + dc, 2)
                visit(2 * to_r + to_c, to_r, 2 * z + to_c)

    def relay_in():
        @pl.loop(0, nz // 2, unroll=few)
        def _(k):
            pair = jnp.concatenate([zr_buf[2 * k + i].reshape(half * nr, 128) for i in range(2)], axis=1)
            out = mm(spread_in[...], pair)
            for i in range(2):
                zt_buf[:, 2 * k + i] = out[:, 128 * i : 128 * i + 128].reshape(2 * nr, blk, 128).astype(BF)

    def send_in_plane(t):
        to_r = moved(t // 2)
        to_c = lax.rem(core + t, 2)
        landing = v_buf.at[1, pl.ds(rep * nf + core * nz, nz)]
        if isinstance(t, int):
            pltpu.make_async_copy(zt_buf.at[2 * rep + core], landing, in_recv.at[1]).start()
        else:
            pltpu.make_async_remote_copy(
                zt_buf.at[2 * to_r + to_c], landing, p_send, in_recv.at[1],
                device_id=(to_r, 2 * z + to_c), device_id_type=MESH,
            ).start()

    def plane_out():
        def send(to, to_r, to_f):
            pltpu.make_async_remote_copy(
                w_buf.at[1, pl.ds(to * nz, nz)], zv_buf.at[2 * rep + core], po_send, po_recv,
                device_id=(to_r, to_f), device_id_type=MESH,
            ).start()

        pltpu.make_async_copy(w_buf.at[1, pl.ds((2 * rep + core) * nz, nz)], zv_buf.at[2 * rep + core], po_recv).start()
        in_plane(send)

    def relay_out():
        @pl.loop(0, nz // 2, unroll=few)
        def _(k):
            pair = jnp.concatenate(
                [zv_buf[:, 2 * k + i].reshape(2 * nr * blk, 128) for i in range(2)], axis=1
            )
            out = mm(spread_out[...], pair).astype(BF)
            for i in range(2):
                zs_buf[2 * k + i] = out[:, 128 * i : 128 * i + 128].reshape(half, nr, 128)

    def unpack(second):
        chosen = jnp.concatenate([select(0), select(1)], axis=0)

        @pl.loop(0, half // 2, unroll=half // 2 if relayed else 1)
        def _(k):
            tiles = [
                jnp.concatenate([s_buf[0, :, 2 * k + i].reshape(mats, 128), second(2 * k + i)], axis=0) for i in range(2)
            ]
            out = mm(jnp.concatenate(tiles, axis=1), chosen, ((0,), (0,))).astype(BF)
            for i in range(2):
                upd_ref[2 * k + i] = out[128 * i : 128 * i + 64]
                upd_ref[2 * k + i + half] = out[128 * i + 64 : 128 * i + 128]

    def all_but_one(ref):
        return ref.at[pl.ds(0, ref.shape[0] - 1)]

    loads[0].wait()
    if relayed:
        gather(1)
        pl.semaphore_wait(barrier, mats - 1)
        along_z(zs_buf, zr_buf, z_send, z_recv)
        gather(0)
        for load in loads[1:]:
            load.wait()
        regroup_all(0)
        relay_matrices()
        spin_momentum(1)
        spin_momentum(0)

        wait_bytes(zr_buf, z_recv)
        relay_in()
        send_in_plane(0)

        @pl.loop(1, 2 * nr)
        def _(t):
            send_in_plane(t)

        send_in(0, True)
        wait_bytes(v_buf.at[1], in_recv.at[1])
        orthogonalize(1)
        plane_out()

        wait_bytes(v_buf.at[0], in_recv.at[0])
        orthogonalize(0)
        send_out(0)

        wait_bytes(zv_buf, po_recv)
        wait_bytes(all_but_one(zs_buf), z_send)
        relay_out()
        along_z(zs_buf, zu_buf, zo_send, zo_recv)
        store_momentum(1)
        store_momentum(0)

        ungroup(0)
        wait_bytes(zu_buf, zo_recv)
        unpack(lambda a: zu_buf[:, a].reshape(nz * nr, 128))
        wait_bytes(all_but_one(zt_buf), p_send)
        wait_bytes(all_but_one(zv_buf), po_send)
        wait_bytes(all_but_one(zs_buf), zo_send)
    else:
        gather(0)
        for load in loads[1:]:
            load.wait()
        pl.semaphore_wait(barrier, mats - 1)
        send_in(0, False)
        gather(1)
        send_in(1, False)
        spin_momentum(0)
        spin_momentum(1)
        for s in range(2):
            wait_bytes(v_buf.at[s], in_recv.at[s])
            orthogonalize(s)
            send_out(s)
        for s in range(2):
            store_momentum(s)
        for s in range(2):
            ungroup(s)
        unpack(lambda a: s_buf[1, :, a].reshape(mats, 128))

    for s in range(2):
        wait_bytes(new.at[s], new_sem.at[s])
    for s in range(1 if relayed else 2):
        wait_bytes(all_but_one(t_buf.at[s]), in_send.at[s])
        wait_bytes(all_but_one(w_buf.at[s]), out_send.at[s])


def one_hot(rows, cols, pairs):
    out = np.zeros((rows, cols), np.float32)
    for i, j in pairs:
        out[i, j] = 1.0
    return jnp.asarray(out, BF)


def on_device(grads, momentum, owner):
    nf, nr = lax.axis_size("fsdp"), lax.axis_size("rep")
    mats, tile_rows, tile_cols = grads.shape
    half = tile_rows // 2
    hid, width = nf * tile_rows, nr * tile_cols
    blk = half + 2
    upper = nf * blk
    pad = 2 * upper
    nz = nf // 2

    regroup_pairs = [(r * blk + a, a * nr + r) for r in range(nr) for a in range(half)]
    row_pairs = [
        (tile_rows * f + half * h + a, h * upper + (f % 2 * nz + f // 2) * blk + a)
        for f in range(nf) for h in range(2) for a in range(half)
    ]
    swap_pairs = [(i * 128 + j * 64 + c, j * 128 + i * 64 + c) for i in range(2) for j in range(2) for c in range(64)]
    flip = lambda pairs: [(j, i) for i, j in pairs]
    regroup = one_hot(nr * blk, half * nr, regroup_pairs)
    regroup_t = one_hot(half * nr, nr * blk, flip(regroup_pairs))
    rows = one_hot(pad, pad, row_pairs)
    rows_t = one_hot(pad, pad, flip(row_pairs))
    swap = one_hot(256, 256, swap_pairs)

    vmem = pl.BlockSpec(memory_space=pltpu.VMEM)
    hbm = pl.BlockSpec(memory_space=pl.ANY)
    cfg = (nr, nf, half, hid, width, pad)
    turned = grads.transpose(1, 2, 0)
    tables = [regroup, regroup_t, rows, rows_t, swap]
    by_f = pltpu.VMEM((2, nf, half, nr, 128), BF)
    tiles = pltpu.VMEM((2, mats, blk, 128), BF)
    by_z = pltpu.VMEM((nz, half, nr, 128), BF)
    in_plane = pltpu.VMEM((2 * nr, nz, blk, 128), BF)
    one = pltpu.SemaphoreType.DMA(())
    relay_scratch = [
        by_z, by_z, in_plane, in_plane, by_z,
        pltpu.VMEM((2 * nr * blk, half * nr), BF),
        pltpu.VMEM((half * nr, 2 * nr * blk), BF),
        *[one for _ in range(7)],
    ]

    def run(relayed, operands):
        return pl.pallas_call(
            functools.partial(kernel, cfg, relayed),
            out_shape=(
                jax.ShapeDtypeStruct((tile_rows, tile_cols, mats), BF),
                jax.ShapeDtypeStruct(momentum.shape[1:], BF),
            ),
            in_specs=[vmem] + [hbm] * 7,
            out_specs=(vmem, hbm),
            scratch_shapes=[
                pltpu.VMEM(turned.shape, BF),
                *[pltpu.VMEM(table.shape, BF) for table in tables],
                pltpu.VMEM((2, mats), jnp.int32),
                by_f, tiles, tiles, tiles, tiles,
                pltpu.VMEM((2, pad, width), BF),
                pltpu.VMEM((2, pad, width), BF),
                pltpu.VMEM((2, hid, width), BF),
                pltpu.VMEM((pad, width), F32),
                pltpu.VMEM((pad, width), BF),
                pltpu.VMEM((pad, pad), BF),
                pltpu.VMEM((pad, pad), BF),
                pltpu.SemaphoreType.DMA((6,)),
                *[pltpu.SemaphoreType.DMA((2,)) for _ in range(5)],
                pltpu.SemaphoreType.DMA((2, nz)),
                *(relay_scratch if relayed else []),
            ],
            compiler_params=pltpu.CompilerParams(
                collective_id=1 if relayed else 0, has_side_effects=True, vmem_limit_bytes=58 * 1024 * 1024
            ),
            name="muon_relayed" if relayed else "muon_direct",
        )(*operands)

    order = jnp.arange(mats, dtype=jnp.int32)
    second = (owner[:, None] == owner[None, :]) & (order[:, None] < order[None, :])
    plane = (owner % nf) // 2
    in_each = second[None] & (plane[None, None, :] == jnp.arange(nz, dtype=jnp.int32)[:, None, None])
    fits = jnp.max(jnp.sum(in_each.astype(jnp.int32), axis=(1, 2))) <= nr
    operands = (owner[None, :], turned, momentum[0], *tables)
    update, new = lax.cond(fits, functools.partial(run, True), functools.partial(run, False), operands)
    return (update.transpose(2, 0, 1), new[None])


def solution(mesh):
    return jax.shard_map(
        on_device,
        mesh=mesh,
        in_specs=(P(None, "fsdp", "rep"), P(("rep", "fsdp"), None, None, None), P()),
        out_specs=(P(None, "fsdp", "rep"), P(("rep", "fsdp"), None, None, None)),
        check_vma=False,
    )
```

```python
import functools

import jax
import jax.numpy as jnp
import numpy as np
from jax import lax
from jax.experimental import pallas as pl
from jax.experimental.pallas import tpu as pltpu
from jax.sharding import PartitionSpec as P

ITERS = 2
MESH = pl.DeviceIdType.MESH
BF = jnp.bfloat16
F32 = jnp.float32


def mm(a, b, dims=((1,), (0,))):
    return lax.dot_general(a, b, (dims, ((), ())), preferred_element_type=F32)


def wait_bytes(ref, sem):
    pltpu.make_async_copy(ref, ref, sem).wait()


def tile_cols(n, size):
    return pl.ds(pl.multiple_of(n * size, size), size)


def kernel(
    cfg, relayed,
    owner_ref, g_hbm, mom_hbm, regroup_hbm, regroup_t_hbm, rows_hbm, rows_t_hbm, swap_hbm,
    upd_ref, new_hbm,
    g, regroup, regroup_t, rows, rows_t, swap, keys,
    s_buf, t_buf, v_buf, w_buf, u_buf, mom, spun, new, nest, x, gram, mixed,
    load_sem, mom_sem, new_sem, in_send, in_recv, out_send, out_recv,
    *relay_refs,
):
    nr, nf, half, hid, width, pad = cfg
    rep, fs = lax.axis_index("rep"), lax.axis_index("fsdp")
    mats = nr * nf
    blk = half + 2
    upper = nf * blk
    nz = nf // 2
    z, core = fs // 2, lax.rem(fs, 2)
    lane = rep * nf + core * nz + z
    if relayed:
        (zs_buf, zr_buf, zt_buf, zv_buf, zu_buf, spread_in, spread_out,
         z_send, z_recv, p_send, zo_send, zo_recv, po_send, po_recv) = relay_refs

    loads = [(g_hbm, g), (regroup_hbm, regroup), (swap_hbm, swap), (rows_hbm, rows),
             (rows_t_hbm, rows_t), (regroup_t_hbm, regroup_t)]
    loads = [pltpu.make_async_copy(a, b, load_sem.at[i]) for i, (a, b) in enumerate(loads)]
    for load in loads:
        load.start()
    for s in range(2):
        pltpu.make_async_copy(mom_hbm.at[s], mom.at[s, pl.ds(0, hid)], mom_sem.at[s]).start()

    side = 4
    rx, ry = rep // side, lax.rem(rep, side)

    def moved(j):
        return lax.rem(rx + j, side) * side + lax.rem(ry + j // side + j, side)

    def faces(dz, dc):
        return 2 * lax.rem(z + dz, nz) + lax.rem(core + dc, 2)

    def everyone(visit):
        def four(k, j):
            to_r = moved(j)
            for dc in range(2):
                visit(to_r, faces(k + 1, dc))
                visit(to_r, faces(nz - 1 - k, dc))

        @pl.loop(0, nz // 2 - 1)
        def _(k):
            @pl.loop(0, nr)
            def _(j):
                four(k, j)

        for dc in range(2):
            visit(rep, faces(nz // 2, dc))
        visit(rep, faces(0, 1))

        @pl.loop(1, nr)
        def _(j):
            to_r = moved(j)
            for dc in range(2):
                visit(to_r, faces(nz // 2, dc))
                visit(to_r, faces(0, dc))

    barrier = pltpu.get_barrier_semaphore()

    def greet(to_r, to_f):
        pl.semaphore_signal(barrier, inc=1, device_id=(to_r, to_f), device_id_type=MESH)

    everyone(greet)

    owner = owner_ref[...]
    down = jnp.transpose(jnp.broadcast_to(owner, (mats, mats)))
    index = lax.broadcasted_iota(jnp.int32, (mats, mats), 0)
    order = lax.broadcasted_iota(jnp.int32, (mats, mats), 1)
    earlier = (down == owner) & (index < order)
    slot = jnp.sum(jnp.where(earlier, 1, 0), axis=0, keepdims=True)
    place = (owner % nf) * nr + owner // nf
    keys[0:1, :] = jnp.where(slot == 0, place, -1)
    if relayed:
        plane = jnp.where(slot == 1, (owner % nf) // 2, -1)
        plane_down = jnp.transpose(jnp.broadcast_to(plane, (mats, mats)))
        before = (plane_down == plane) & (index < order)
        rank = jnp.sum(jnp.where(before, 1, 0), axis=0, keepdims=True)
        keys[1:2, :] = jnp.where(slot == 1, plane * nr + rank, -1)
    else:
        keys[1:2, :] = jnp.where(slot == 1, place, -1)

    def relay_matrices():
        member = (owner // nf) * 2 + owner % 2 + 1
        wide = half * nr
        column = lax.broadcasted_iota(jnp.int32, (wide, mats), 0) % nr
        here = jnp.where(keys[1:2, :] == z * nr + column, 1.0, 0.0).astype(BF)
        members = jnp.broadcast_to(member, (8, mats)).astype(F32).astype(BF)
        owner_of = mm(members, here, ((1,), (1,)))[0:1, :]
        line = lax.broadcasted_iota(jnp.int32, (2 * nr * blk, wide), 0)
        source = lax.broadcasted_iota(jnp.int32, (2 * nr * blk, wide), 1)
        wanted = (owner_of == (line // blk + 1).astype(F32)) & (line % blk == source // nr)
        wanted = jnp.where(wanted, 1.0, 0.0)
        spread_in[...] = wanted.astype(BF)
        spread_out[...] = jnp.transpose(wanted).astype(BF)

    few = 4 if relayed else 1

    def select(s):
        places = nz * nr if relayed and s == 1 else mats
        slot_id = lax.broadcasted_iota(jnp.int32, (places, mats), 0)
        return jnp.where(slot_id == keys[s : s + 1, :], 1.0, 0.0).astype(BF)

    def gather(s):
        chosen = select(s)

        @pl.loop(0, half // 2, unroll=half // 2 if relayed else 1)
        def _(k):
            both = jnp.concatenate([g[2 * k], g[2 * k + half], g[2 * k + 1], g[2 * k + 1 + half]], axis=0)
            out = mm(chosen, both, ((1,), (1,))).astype(BF)
            for i in range(2):
                part = out[:, 128 * i : 128 * i + 128]
                if relayed and s == 1:
                    zs_buf[:, 2 * k + i] = part.reshape(nz, nr, 128)
                else:
                    s_buf[s, :, 2 * k + i] = part.reshape(nf, nr, 128)

    def regroup_two(s, k):
        first, second = k, k + 1
        pair = jnp.concatenate(
            [s_buf[s, first].reshape(half * nr, 128), s_buf[s, second].reshape(half * nr, 128)], axis=1
        )
        out = mm(regroup[...], pair)
        t_buf[s, pl.ds(first * nr, nr)] = out[:, :128].reshape(nr, blk, 128).astype(BF)
        t_buf[s, pl.ds(second * nr, nr)] = out[:, 128:].reshape(nr, blk, 128).astype(BF)

    def regroup_all(s):
        @pl.loop(0, nf // 2, unroll=few)
        def _(k):
            regroup_two(s, 2 * k)

    def send_in(s, regrouped):
        def send(to_r, to_f):
            pltpu.make_async_remote_copy(
                t_buf.at[s, to_f * nr + to_r], v_buf.at[s, lane], in_send.at[s], in_recv.at[s],
                device_id=(to_r, to_f), device_id_type=MESH,
            ).start()

        if not regrouped:
            regroup_all(s)
        pltpu.make_async_copy(t_buf.at[s, fs * nr + rep], v_buf.at[s, lane], in_recv.at[s]).start()
        everyone(send)

    def send_out(s):
        def send(to_r, to_f):
            pltpu.make_async_remote_copy(
                w_buf.at[s, to_r * nf + lax.rem(to_f, 2) * nz + to_f // 2], u_buf.at[s, fs * nr + rep], out_send.at[s], out_recv.at[s, z],
                device_id=(to_r, to_f), device_id_type=MESH,
            ).start()

        pltpu.make_async_copy(w_buf.at[s, lane], u_buf.at[s, fs * nr + rep], out_recv.at[s, z]).start()
        everyone(send)

    def spin_momentum(s):
        wait_bytes(mom.at[s, pl.ds(0, hid)], mom_sem.at[s])
        if pad > hid:
            mom[s, hid:pad, :] = jnp.zeros((pad - hid, width), BF)

        @pl.loop(0, width // 256)
        def _(n):
            cols = tile_cols(n, 256)
            spun[s, :, cols] = mm(rows_t[...], mom[s, :, cols]).astype(BF)

    def store_momentum(s):
        own = rep * nf + fs
        mine = jnp.sum(jnp.where(owner_ref[...] == own, 1, 0), axis=1, keepdims=True)
        owned = mine > s

        @pl.loop(0, width // 256)
        def _(n):
            cols = tile_cols(n, 256)
            moment = mm(rows[0:hid, :], spun[s, :, cols])
            new[s, :, cols] = jnp.where(owned, moment, mom[s, 0:hid, cols].astype(F32)).astype(BF)

        pltpu.make_async_copy(new.at[s], new_hbm.at[s], new_sem.at[s]).start()

    def orthogonalize(s):
        def start(q, total):
            pair = jnp.concatenate(
                [v_buf[s, pl.ds((2 * q + i) * nf, nf)].reshape(upper, 128) for i in range(2)], axis=1
            )
            both = mm(pair, swap[...])
            cols = tile_cols(q, 128)
            for h in range(2):
                part = slice(h * upper, (h + 1) * upper)
                grad = both[:, 128 * h : 128 * h + 128]
                moment = (0.95 * spun[s, part, cols].astype(F32) + grad).astype(BF)
                spun[s, part, cols] = moment
                value = grad + 0.95 * moment.astype(F32)
                nest[part, cols] = value
                total = total + jnp.sum(value * value, axis=0, keepdims=True)
            return total

        total = lax.fori_loop(0, width // 128, start, jnp.zeros((1, 128), F32), unroll=2 * few)
        scale = 1.0 / (jnp.sqrt(jnp.sum(total, axis=1, keepdims=True)) + 1e-07)

        @pl.loop(0, width // 256, unroll=few)
        def _(n):
            cols = tile_cols(n, 256)
            x[:, cols] = (nest[:, cols] * scale).astype(BF)

        @pl.loop(0, ITERS)
        def _(turn):
            def columns(count, step):
                if relayed:
                    for n in range(count):
                        step(slice(256 * n, 256 * n + 256))
                else:
                    pl.loop(0, count)(lambda n: step(tile_cols(n, 256)))

            def mirror(ref, cols, part):
                lines = slice(cols.start, pad)
                ref[lines, cols] = part.astype(BF)
                if cols.stop < pad:
                    ref[cols, cols.stop : pad] = jnp.transpose(part[256:]).astype(BF)

            def to_gram(cols):
                if relayed:
                    mirror(gram, cols, mm(x[cols.start :, :], x[cols, :], ((1,), (1,))))
                else:
                    gram[:, cols] = mm(x[...], x[cols, :], ((1,), (1,))).astype(BF)

            def to_mixed(cols):
                lines = slice(cols.start if relayed else 0, pad)
                part = -4.775 * gram[lines, cols].astype(F32) + 2.0315 * mm(gram[lines, :], gram[:, cols])
                if relayed:
                    mirror(mixed, cols, part)
                else:
                    mixed[:, cols] = part.astype(BF)

            def to_x(cols):
                part = x[:, cols]
                product = mm(mixed[...], part)
                x[:, cols] = (3.4445 * part.astype(F32) + product).astype(BF)

            columns(pad // 256, to_gram)
            columns(pad // 256, to_mixed)
            columns(width // 256, to_x)

        factor = 0.2 * max(hid, width) ** 0.5

        @pl.loop(0, nr // 2, unroll=2 * few)
        def _(q):
            cols = tile_cols(q, 128)
            both = jnp.concatenate(
                [(factor * x[h * upper : (h + 1) * upper, cols].astype(F32)).astype(BF) for h in range(2)], axis=1
            )
            out = mm(both, swap[...])
            for i in range(2):
                w_buf[s, pl.ds((2 * q + i) * nf, nf)] = (
                    out[:, 128 * i : 128 * i + 128].reshape(nf, blk, 128).astype(BF)
                )

    def ungroup(s):
        def one(dz):
            k = lax.rem(z + dz, nz)
            wait_bytes(u_buf.at[s, pl.ds(2 * k * nr, 2 * nr)], out_recv.at[s, k])
            pair = jnp.concatenate(
                [u_buf[s, pl.ds((2 * k + i) * nr, nr)].reshape(nr * blk, 128) for i in range(2)], axis=1
            )
            out = mm(regroup_t[...], pair).astype(BF)
            s_buf[s, 2 * k] = out[:, :128].reshape(half, nr, 128)
            s_buf[s, 2 * k + 1] = out[:, 128:].reshape(half, nr, 128)

        @pl.loop(0, nz // 2 - 1)
        def _(k):
            one(k + 1)
            one(nz - 1 - k)

        @pl.loop(0, 2)
        def _(k):
            one(k * (nz // 2))

    def along_z(src, dst, send_sem, recv_sem):
        pltpu.make_async_copy(src.at[z], dst.at[z], recv_sem).start()

        def send(dz):
            to_z = lax.rem(z + dz, nz)
            pltpu.make_async_remote_copy(
                src.at[to_z], dst.at[z], send_sem, recv_sem,
                device_id=(rep, 2 * to_z + core), device_id_type=MESH,
            ).start()

        send(nz // 2)
        for k in range(nz // 2 - 1, 0, -1):
            send(k)
            send(nz - k)

    def in_plane(visit):
        visit(2 * rep + 1 - core, rep, 2 * z + 1 - core)

        @pl.loop(1, nr)
        def _(j):
            to_r = moved(j)
            for dc in range(2):
                to_c = lax.rem(core + dc, 2)
                visit(2 * to_r + to_c, to_r, 2 * z + to_c)

    def relay_in():
        @pl.loop(0, nz // 2, unroll=few)
        def _(k):
            pair = jnp.concatenate([zr_buf[2 * k + i].reshape(half * nr, 128) for i in range(2)], axis=1)
            out = mm(spread_in[...], pair)
            for i in range(2):
                zt_buf[:, 2 * k + i] = out[:, 128 * i : 128 * i + 128].reshape(2 * nr, blk, 128).astype(BF)

    def send_in_plane(t):
        to_r = moved(t // 2)
        to_c = lax.rem(core + t, 2)
        landing = v_buf.at[1, pl.ds(rep * nf + core * nz, nz)]
        if isinstance(t, int):
            pltpu.make_async_copy(zt_buf.at[2 * rep + core], landing, in_recv.at[1]).start()
        else:
            pltpu.make_async_remote_copy(
                zt_buf.at[2 * to_r + to_c], landing, p_send, in_recv.at[1],
                device_id=(to_r, 2 * z + to_c), device_id_type=MESH,
            ).start()

    def plane_out():
        def send(to, to_r, to_f):
            pltpu.make_async_remote_copy(
                w_buf.at[1, pl.ds(to * nz, nz)], zv_buf.at[2 * rep + core], po_send, po_recv,
                device_id=(to_r, to_f), device_id_type=MESH,
            ).start()

        pltpu.make_async_copy(w_buf.at[1, pl.ds((2 * rep + core) * nz, nz)], zv_buf.at[2 * rep + core], po_recv).start()
        in_plane(send)

    def relay_out():
        @pl.loop(0, nz // 2, unroll=few)
        def _(k):
            pair = jnp.concatenate(
                [zv_buf[:, 2 * k + i].reshape(2 * nr * blk, 128) for i in range(2)], axis=1
            )
            out = mm(spread_out[...], pair).astype(BF)
            for i in range(2):
                zs_buf[2 * k + i] = out[:, 128 * i : 128 * i + 128].reshape(half, nr, 128)

    def unpack(second):
        chosen = jnp.concatenate([select(0), select(1)], axis=0)

        @pl.loop(0, half // 2, unroll=half // 2 if relayed else 1)
        def _(k):
            tiles = [
                jnp.concatenate([s_buf[0, :, 2 * k + i].reshape(mats, 128), second(2 * k + i)], axis=0) for i in range(2)
            ]
            out = mm(jnp.concatenate(tiles, axis=1), chosen, ((0,), (0,))).astype(BF)
            for i in range(2):
                upd_ref[2 * k + i] = out[128 * i : 128 * i + 64]
                upd_ref[2 * k + i + half] = out[128 * i + 64 : 128 * i + 128]

    def all_but_one(ref):
        return ref.at[pl.ds(0, ref.shape[0] - 1)]

    loads[0].wait()
    if relayed:
        gather(1)
        pl.semaphore_wait(barrier, mats - 1)
        along_z(zs_buf, zr_buf, z_send, z_recv)
        gather(0)
        for load in loads[1:]:
            load.wait()
        regroup_all(0)
        relay_matrices()
        spin_momentum(1)
        spin_momentum(0)

        wait_bytes(zr_buf, z_recv)
        relay_in()
        send_in_plane(0)

        @pl.loop(1, 2 * nr)
        def _(t):
            send_in_plane(t)

        send_in(0, True)
        wait_bytes(v_buf.at[1], in_recv.at[1])
        orthogonalize(1)
        plane_out()

        wait_bytes(v_buf.at[0], in_recv.at[0])
        orthogonalize(0)
        send_out(0)

        wait_bytes(zv_buf, po_recv)
        wait_bytes(all_but_one(zs_buf), z_send)
        relay_out()
        along_z(zs_buf, zu_buf, zo_send, zo_recv)
        store_momentum(1)
        store_momentum(0)

        ungroup(0)
        wait_bytes(zu_buf, zo_recv)
        unpack(lambda a: zu_buf[:, a].reshape(nz * nr, 128))
        wait_bytes(all_but_one(zt_buf), p_send)
        wait_bytes(all_but_one(zv_buf), po_send)
        wait_bytes(all_but_one(zs_buf), zo_send)
    else:
        gather(0)
        for load in loads[1:]:
            load.wait()
        pl.semaphore_wait(barrier, mats - 1)
        send_in(0, False)
        gather(1)
        send_in(1, False)
        spin_momentum(0)
        spin_momentum(1)
        for s in range(2):
            wait_bytes(v_buf.at[s], in_recv.at[s])
            orthogonalize(s)
            send_out(s)
        for s in range(2):
            store_momentum(s)
        for s in range(2):
            ungroup(s)
        unpack(lambda a: s_buf[1, :, a].reshape(mats, 128))

    for s in range(2):
        wait_bytes(new.at[s], new_sem.at[s])
    for s in range(1 if relayed else 2):
        wait_bytes(all_but_one(t_buf.at[s]), in_send.at[s])
        wait_bytes(all_but_one(w_buf.at[s]), out_send.at[s])


def one_hot(rows, cols, pairs):
    out = np.zeros((rows, cols), np.float32)
    for i, j in pairs:
        out[i, j] = 1.0
    return jnp.asarray(out, BF)


def on_device(grads, momentum, owner):
    nf, nr = lax.axis_size("fsdp"), lax.axis_size("rep")
    mats, tile_rows, tile_cols = grads.shape
    half = tile_rows // 2
    hid, width = nf * tile_rows, nr * tile_cols
    blk = half + 2
    upper = nf * blk
    pad = 2 * upper
    nz = nf // 2

    regroup_pairs = [(r * blk + a, a * nr + r) for r in range(nr) for a in range(half)]
    row_pairs = [
        (tile_rows * f + half * h + a, h * upper + (f % 2 * nz + f // 2) * blk + a)
        for f in range(nf) for h in range(2) for a in range(half)
    ]
    swap_pairs = [(i * 128 + j * 64 + c, j * 128 + i * 64 + c) for i in range(2) for j in range(2) for c in range(64)]
    flip = lambda pairs: [(j, i) for i, j in pairs]
    regroup = one_hot(nr * blk, half * nr, regroup_pairs)
    regroup_t = one_hot(half * nr, nr * blk, flip(regroup_pairs))
    rows = one_hot(pad, pad, row_pairs)
    rows_t = one_hot(pad, pad, flip(row_pairs))
    swap = one_hot(256, 256, swap_pairs)

    vmem = pl.BlockSpec(memory_space=pltpu.VMEM)
    hbm = pl.BlockSpec(memory_space=pl.ANY)
    cfg = (nr, nf, half, hid, width, pad)
    turned = grads.transpose(1, 2, 0)
    tables = [regroup, regroup_t, rows, rows_t, swap]
    by_f = pltpu.VMEM((2, nf, half, nr, 128), BF)
    tiles = pltpu.VMEM((2, mats, blk, 128), BF)
    by_z = pltpu.VMEM((nz, half, nr, 128), BF)
    in_plane = pltpu.VMEM((2 * nr, nz, blk, 128), BF)
    one = pltpu.SemaphoreType.DMA(())
    relay_scratch = [
        by_z, by_z, in_plane, in_plane, by_z,
        pltpu.VMEM((2 * nr * blk, half * nr), BF),
        pltpu.VMEM((half * nr, 2 * nr * blk), BF),
        *[one for _ in range(7)],
    ]

    def run(relayed, operands):
        return pl.pallas_call(
            functools.partial(kernel, cfg, relayed),
            out_shape=(
                jax.ShapeDtypeStruct((tile_rows, tile_cols, mats), BF),
                jax.ShapeDtypeStruct(momentum.shape[1:], BF),
            ),
            in_specs=[vmem] + [hbm] * 7,
            out_specs=(vmem, hbm),
            scratch_shapes=[
                pltpu.VMEM(turned.shape, BF),
                *[pltpu.VMEM(table.shape, BF) for table in tables],
                pltpu.VMEM((2, mats), jnp.int32),
                by_f, tiles, tiles, tiles, tiles,
                pltpu.VMEM((2, pad, width), BF),
                pltpu.VMEM((2, pad, width), BF),
                pltpu.VMEM((2, hid, width), BF),
                pltpu.VMEM((pad, width), F32),
                pltpu.VMEM((pad, width), BF),
                pltpu.VMEM((pad, pad), BF),
                pltpu.VMEM((pad, pad), BF),
                pltpu.SemaphoreType.DMA((6,)),
                *[pltpu.SemaphoreType.DMA((2,)) for _ in range(5)],
                pltpu.SemaphoreType.DMA((2, nz)),
                *(relay_scratch if relayed else []),
            ],
            compiler_params=pltpu.CompilerParams(
                collective_id=1 if relayed else 0, has_side_effects=True, vmem_limit_bytes=58 * 1024 * 1024
            ),
            name="muon_relayed" if relayed else "muon_direct",
        )(*operands)

    order = jnp.arange(mats, dtype=jnp.int32)
    second = (owner[:, None] == owner[None, :]) & (order[:, None] < order[None, :])
    plane = (owner % nf) // 2
    in_each = second[None] & (plane[None, None, :] == jnp.arange(nz, dtype=jnp.int32)[:, None, None])
    fits = jnp.max(jnp.sum(in_each.astype(jnp.int32), axis=(1, 2))) <= nr
    operands = (owner[None, :], turned, momentum[0], *tables)
    update, new = lax.cond(fits, functools.partial(run, True), functools.partial(run, False), operands)
    return (update.transpose(2, 0, 1), new[None])


def solution(mesh):
    return jax.shard_map(
        on_device,
        mesh=mesh,
        in_specs=(P(None, "fsdp", "rep"), P(("rep", "fsdp"), None, None, None), P()),
        out_specs=(P(None, "fsdp", "rep"), P(("rep", "fsdp"), None, None, None)),
        check_vma=False,
    )
```
